32 devices in a mesh: mesh: 4 (over y, x), harm: 8 (over z, core).
Axes of the slice: x: 2, y: 2, z: 4, core: 2. Of those that a mesh axis runs over, the one named last changes fastest.
Arguments:
- current_pattern: float32 [128, 4096], P('mesh'), may hold values from -6 to 6
- conductivity: float32 [128, 4096], P('mesh'), may hold values from 0.5 to 8
- cooling: float32 [128, 4096], P('mesh'), may hold values from 0.05 to 0.5
- harm_order: int32 [8], P('harm'), may hold values from 8 to 64
- harm_amp: int32 [8], P('harm'), may hold values from 1 to 4
- block_counts: int32 [8], P('harm'), may hold values from 1 to 32, as said below
Outputs:
- averaged_dissipation: float32 [128, 4096], P('mesh', 'harm')
- thermal_increase: float32 [128, 4096], P('mesh', 'harm')
The draws below stay inside these ranges and needn't reach their ends.
Inputs may be any that keep to these rules, and one draw needn't show every extreme that they name: `block_counts`: some harmonic has block count 32.
All inputs are finite; a program needn't handle non-finite values.
Results may differ from the reference program's by a relative error of at most 0.00002.
Values sent between devices are 32-bit elements; how exact they have to be, the bound alone decides.
No kernel may reach another device: no remote copies, remote signals or barrier semaphores. Data moves between devices by JAX's collectives and lax.ppermute only.
A program may use at most 64 MiB of HBM per device.

```python
import math
import jax
import jax.numpy as jnp
from jax import lax

L = 4096
BLK = 128
EDDY_SWEEPS = 3
HEAT_SWEEPS = 4
NBLK = 32
HARMS = 8
NX = 128


def draw_block_counts(key, part):
    first, second = jax.random.split(jax.random.fold_in(key, 7))
    counts = jax.random.randint(first, (HARMS,), 1, NBLK + 1)
    where = jax.random.randint(second, (), 0, HARMS)
    return jnp.where(jnp.arange(HARMS) == where, NBLK, counts).astype(jnp.int32)


def with_ends(values, stream_key, low, largest):
    extent = values.shape
    place = [jax.random.randint(jax.random.fold_in(stream_key, axis), (), 0, extent[axis]) for axis in range(len(extent))]
    values = values.at[tuple(place)].set(low)
    longest = extent.index(max(extent))
    place[longest] = (place[longest] + 1) % extent[longest]
    return values.at[tuple(place)].set(largest)


def block_scale(key, extent, cuts, least, high):
    def one(dim, parts):
        heights = jax.random.uniform(jax.random.fold_in(jax.random.fold_in(key, 6), dim), (parts,), jnp.float32, least / len(cuts), high / len(cuts))
        return jnp.repeat(jnp.exp(heights), extent[dim] // parts).reshape((-1,) + (1,) * (len(extent) - dim - 1))

    gain = one(*cuts[0])
    for cut in cuts[1:]:
        gain = gain * one(*cut)
    return gain


def scatter_about(stream_key, shape, spread, limit, shards=(), held_as=jnp.bfloat16):
    entries = spread * jax.random.normal(stream_key, shape, jnp.float32)
    if shards:
        entries = entries * block_scale(stream_key, shape, shards, -0.22, 0.18)
    return jnp.clip(entries, -limit, limit).astype(held_as)


def setup_inputs(seed: int = 0) -> dict:
    streams_of = jax.random.split(jax.random.key(seed), 7)
    current_pattern = scatter_about(streams_of[0], (NX, L), 1.0, 6.0, ((0, 4),), jnp.float32)
    conductivity = jnp.clip(jnp.exp(math.log(8.0) - 2.7725887 * jax.random.uniform(streams_of[1], (NX, L), jnp.float32) ** block_scale(streams_of[1], (NX, L), ((0, 4),), -0.2, 0.2)), 0.5, 8.0)
    cooling = jnp.clip(jnp.exp(math.log(0.5) - 2.3025851 * jax.random.uniform(streams_of[2], (NX, L), jnp.float32) ** block_scale(streams_of[2], (NX, L), ((0, 4),), -0.2, 0.2)), 0.05, 0.5)
    harm_order = with_ends(jax.random.randint(streams_of[3], (HARMS,), 8, 65), jax.random.fold_in(streams_of[3], 1), 8, 64).astype(jnp.int32)
    harm_amp = with_ends(jax.random.randint(streams_of[4], (HARMS,), 1, 5), jax.random.fold_in(streams_of[4], 1), 1, 4).astype(jnp.int32)
    block_counts = draw_block_counts(jax.random.fold_in(streams_of[6], 71), 0)
    return {"current_pattern": current_pattern, "conductivity": conductivity, "cooling": cooling, "harm_order": harm_order, "harm_amp": harm_amp, "block_counts": block_counts}


base_freq = 0.1


def neighbour_total(field):
    bordered_array = jnp.pad(field, 1)
    return bordered_array[2:, 1:-1] + bordered_array[:-2, 1:-1] + bordered_array[1:-1, 2:] + bordered_array[1:-1, :-2]


def harmonic_loss(current_pattern, conductivity, order, amp, count):
    omega = base_freq * order.astype(jnp.float32)
    columns = jnp.arange(L).astype(jnp.int32)
    mask = (columns < count * BLK).astype(jnp.float32)[None, :]
    source = amp.astype(jnp.float32) * current_pattern * mask
    product = omega * conductivity
    denom = 16.0 + product * product
    inv_re = 4.0 / denom
    inv_im = -product / denom
    real_part = source * inv_re
    imag_part = source * inv_im
    for sweep in range(EDDY_SWEEPS - 1):
        near_re = source + neighbour_total(real_part)
        near_im = neighbour_total(imag_part)
        real_part = mask * (near_re * inv_re - near_im * inv_im)
        imag_part = mask * (near_re * inv_im + near_im * inv_re)
    return 0.5 * omega * omega * conductivity * (real_part * real_part + imag_part * imag_part)


def reference(current_pattern, conductivity, cooling, harm_order, harm_amp, block_counts):
    def accumulate(index, total):
        return total + harmonic_loss(current_pattern, conductivity, harm_order[index], harm_amp[index], block_counts[index])

    total = lax.fori_loop(0, HARMS, accumulate, jnp.zeros(current_pattern.shape, current_pattern.dtype))
    averaged_dissipation = total / HARMS
    inverted_weight = 1.0 / (4.0 + cooling)
    thermal_increase = averaged_dissipation * inverted_weight
    for sweep in range(HEAT_SWEEPS - 1):
        thermal_increase = (averaged_dissipation + neighbour_total(thermal_increase)) * inverted_weight
    return averaged_dissipation, thermal_increase
```

```python
import functools

import jax
import jax.numpy as jnp
from jax import lax
from jax.experimental import pallas as pl
from jax.experimental.pallas import tpu as pltpu
from jax.sharding import PartitionSpec as P

LANES = 128
HALF = 64
TILE = 8
BASE_FREQ = 0.1
MARGIN = 5
F32 = jnp.float32


def lane_iota(rows=TILE):
    return lax.broadcasted_iota(jnp.int32, (rows, LANES), 1)


def sublane_iota():
    return lax.broadcasted_iota(jnp.int32, (TILE, LANES), 0)


def side_tile(buf, rows, left, right):
    lanes = lane_iota(rows.size if hasattr(rows, "size") else rows.stop - rows.start)
    after = buf[rows, pl.ds(pl.multiple_of(right, LANES), LANES)]
    before = buf[rows, pl.ds(pl.multiple_of(left, LANES), LANES)]
    return jnp.where(lanes < HALF, after, before)


def window(start, size, total):
    begin = jnp.clip(start - LANES, 0, total - size)
    return pl.multiple_of(begin, LANES)


def pack_kernel(order, amp, count, cur, con, coo, own, other, params, buf, sems, *, width):
    slab, total = cur.shape
    h = lax.axis_index("harm")
    core = lax.rem(h, 2)
    size = buf.shape[2]
    first = (h - core) * width
    begin = window(first, size, total)
    row = pl.multiple_of(jnp.where(core == 0, slab - TILE, 0), TILE)
    copies = [
        pltpu.make_async_copy(
            ref.at[pl.ds(row, TILE), pl.ds(begin, size)], buf.at[i], sems.at[i]
        )
        for i, ref in enumerate((cur, con, coo))
    ]
    for copy in copies:
        copy.start()
    rows = lax.broadcasted_iota(jnp.int32, params.shape, 0)
    lanes = lax.broadcasted_iota(jnp.int32, params.shape, 1)
    value = jnp.where(
        lanes == 0, order[0], jnp.where(lanes == 1, amp[0], count[0])
    ).astype(F32)
    params[...] = jnp.where((rows == h) & (lanes < 3), value, 0.0)
    for copy in copies:
        copy.wait()
    sub = sublane_iota()
    goes_up = core == 0
    shift = jnp.where(goes_up, 3, 5)
    take_cur = jnp.where(goes_up, sub - 3, 4 - sub) >= 0
    for target, out in ((core, own), (1 - core, other)):
        offset = first + target * width - begin
        left = jnp.maximum(offset - LANES, 0)
        right = jnp.minimum(offset + width, size - LANES)
        pieces = []
        for j in range(width // LANES):
            at = pl.ds(pl.multiple_of(offset + j * LANES, LANES), LANES)
            pieces.append([buf[i, :, at] for i in range(3)])
        pieces.append(
            [side_tile(buf.at[i], slice(0, TILE), left, right) for i in range(3)]
        )
        for j, (a, b, c) in enumerate(pieces):
            at = slice(j * LANES, (j + 1) * LANES)
            out[:TILE, at] = jnp.where(take_cur, a, pltpu.roll(c, shift, 0))
            out[TILE:, at] = b


def gather_kernel(cur, con, coo, cur_out, con_out, coo_out, buf, sems, *, width):
    slab, total = cur.shape
    h = lax.axis_index("harm")
    size = buf.shape[2]
    begin = window(h * width, size, total)
    copies = [
        pltpu.make_async_copy(ref.at[:, pl.ds(begin, size)], buf.at[i], sems.at[i])
        for i, ref in enumerate((cur, con, coo))
    ]
    for copy in copies:
        copy.start()
    offset = h * width - begin
    left = jnp.maximum(offset - LANES, 0)
    right = jnp.minimum(offset + width, size - LANES)
    for i, out in enumerate((cur_out, con_out, coo_out)):
        copies[i].wait()
        out[:, :width] = buf[i, :, pl.ds(pl.multiple_of(offset, LANES), width)]
        out[:, width:] = side_tile(buf.at[i], slice(0, slab), left, right)


def sides(tiles, lanes):
    n = len(tiles)
    back = [pltpu.roll(t, 1, 1) for t in tiles]
    fore = [pltpu.roll(t, LANES - 1, 1) for t in tiles]
    return [
        jnp.where(lanes == 0, back[j - 1], back[j])
        + jnp.where(lanes == LANES - 1, fore[(j + 1) % n], fore[j])
        for j in range(n)
    ]


def fold_harmonics(rows, sub):
    level = list(rows)
    for half in (4, 2, 1):
        low = (sub & half) == 0
        merged = []
        for i in range(half):
            a, b = level[i], level[i + half]
            if a is None and b is None:
                merged.append(None)
                continue
            a = jnp.zeros((TILE, LANES), F32) if a is None else a
            b = jnp.zeros((TILE, LANES), F32) if b is None else b
            keep = jnp.where(low, a, b)
            move = jnp.where(low, b, a)
            merged.append(keep + jnp.where(low, pltpu.roll(move, TILE - half, 0), pltpu.roll(move, half, 0)))
        level = merged
    return level[0]


def loss_kernel(
    p0, p1, cur, con, coo, near, far, diss, heat,
    xcur, xcon, xcoo, rr, gg, ss, ra, ha, rb, hb, qq, *, width, harmonics,
):
    slab = cur.shape[0]
    nt = width // LANES + 1
    top, bottom = TILE, TILE + slab
    ext = slab + 2 * TILE
    h = lax.axis_index("harm")
    m = lax.axis_index("mesh")
    last_h = lax.axis_size("harm") - 1
    last_m = lax.axis_size("mesh") - 1
    core = lax.rem(h, 2)
    lanes, sub = lane_iota(), sublane_iota()
    xcur[top:bottom, :] = cur[...]
    xcon[top:bottom, :] = con[...]
    xcoo[top:bottom, :] = coo[...]

    def edges(up, down):
        xcur[0:TILE, :] = up[:TILE, :]
        xcon[0:TILE, :] = up[TILE:, :]
        xcoo[0:TILE, :] = pltpu.roll(up[:TILE, :], TILE - 3, 0)
        xcur[bottom:ext, :] = down[:TILE, :]
        xcon[bottom:ext, :] = down[TILE:, :]
        xcoo[bottom:ext, :] = pltpu.roll(down[:TILE, :], TILE - 5, 0)

    @pl.when(core == 0)
    def _():
        edges(near, far)

    @pl.when(core == 1)
    def _():
        edges(far, near)

    has_up = (m > 0).astype(F32)
    has_down = (m < last_m).astype(F32)
    has_left = (h > 0).astype(F32)
    has_right = (h < last_h).astype(F32)
    col_tile = (h * (width // LANES)).astype(F32)
    zero = jnp.zeros((TILE, LANES), F32)

    for group in range((harmonics + TILE - 1) // TILE):
        at = slice(group * TILE, (group + 1) * TILE)
        par = jnp.maximum(p0[at, :], p1[at, :])
        order = jnp.broadcast_to(par[:, 0:1], (TILE, LANES))
        amp = jnp.broadcast_to(par[:, 1:2], (TILE, LANES))
        count = jnp.broadcast_to(par[:, 2:3], (TILE, LANES))
        omega = BASE_FREQ * order
        quarter = 0.25 * omega
        weight = (0.5 / harmonics) * omega * amp * amp
        masks = [
            jnp.where(count > col_tile + j, 0.25, 0.0) for j in range(nt - 1)
        ]
        masks.append(
            jnp.where(
                lanes < HALF,
                jnp.where(count > col_tile + (nt - 1), 0.25 * has_right, 0.0),
                jnp.where(count > col_tile - 1, 0.25 * has_left, 0.0),
            )
        )

        def start_rows(base, subs, scale):
            scaled = masks if scale is None else [k * scale for k in masks]
            for j in range(nt):
                col = slice(j * LANES, (j + 1) * LANES)
                a = xcur[pl.ds(base, TILE), col]
                b = xcon[pl.ds(base, TILE), col]
                for s in subs:
                    src = jnp.broadcast_to(a[s : s + 1, :], (TILE, LANES))
                    g = quarter * jnp.broadcast_to(b[s : s + 1, :], (TILE, LANES))
                    d = 1.0 + g * g
                    r = pl.reciprocal(d, approx=True)
                    r = r * (2.0 - d * r)
                    r = r * scaled[j]
                    re = src * r
                    rr[base + s, :, col] = r
                    gg[base + s, :, col] = g
                    ss[base + s, :, col] = src
                    ra[base + s, :, col] = re
                    ha[base + s, :, col] = g * re

        start_rows(0, range(TILE - MARGIN, TILE), has_up)
        start_rows(bottom, range(MARGIN), has_down)

        def start_body(i, carry):
            start_rows(pl.multiple_of(top + i * TILE, TILE), range(TILE), None)
            return carry

        lax.fori_loop(0, slab // TILE, start_body, 0)

        def load(ref, row):
            return [ref[row, :, j * LANES : (j + 1) * LANES] for j in range(nt)]

        def near_sum(ref, row):
            mid = sides(load(ref, row), lanes)
            return [
                x + (u + v)
                for x, u, v in zip(mid, load(ref, row - 1), load(ref, row + 1))
            ]

        def sweep_rows(base, subs):
            for s in subs:
                row = base + s
                nr, nh = near_sum(ra, row), near_sum(ha, row)
                r, g, src = load(rr, row), load(gg, row), load(ss, row)
                for j in range(nt):
                    col = slice(j * LANES, (j + 1) * LANES)
                    x = src[j] + nr[j]
                    rb[row, :, col] = r[j] * (x - g[j] * nh[j])
                    hb[row, :, col] = r[j] * (g[j] * x + nh[j])

        def sweep_body(i, carry):
            sweep_rows(TILE - MARGIN + 1 + i * TILE, range(TILE))
            return carry

        lax.fori_loop(0, (slab + 2 * (MARGIN - 1)) // TILE, sweep_body, 0)

        def loss_rows(base, subs):
            rows = [[None] * TILE for _ in range(nt)]
            for s in subs:
                row = base + s
                nr, nh = near_sum(rb, row), near_sum(hb, row)
                r, g, src = load(rr, row), load(gg, row), load(ss, row)
                for j in range(nt):
                    x = src[j] + nr[j]
                    rows[j][s] = (weight * g[j] * r[j]) * (x * x + nh[j] * nh[j])
            for j in range(nt):
                col = slice(j * LANES, (j + 1) * LANES)
                total = fold_harmonics(rows[j], sub)
                if group:
                    total = qq[pl.ds(base, TILE), col] + total
                qq[pl.ds(base, TILE), col] = total

        loss_rows(0, range(TILE - MARGIN + 2, TILE))
        loss_rows(bottom, range(MARGIN - 2))

        def loss_body(i, carry):
            loss_rows(pl.multiple_of(top + i * TILE, TILE), range(TILE))
            return carry

        lax.fori_loop(0, slab // TILE, loss_body, 0)

    ntile = ext // TILE
    side = jnp.where(lanes < HALF, has_right, has_left)
    q = [[qq[i * TILE : (i + 1) * TILE, j * LANES : (j + 1) * LANES] for j in range(nt)] for i in range(ntile)]
    rec = []
    for i in range(ntile):
        line = []
        for j in range(nt):
            w = 1.0 / (4.0 + xcoo[i * TILE : (i + 1) * TILE, j * LANES : (j + 1) * LANES])
            if i == 0:
                w = w * has_up
            if i == ntile - 1:
                w = w * has_down
            if j == nt - 1:
                w = w * side
            line.append(w)
        rec.append(line)
    t = [[q[i][j] * rec[i][j] for j in range(nt)] for i in range(ntile)]
    for _ in range(3):
        back = [[pltpu.roll(x, 1, 0) for x in line] for line in t]
        fore = [[pltpu.roll(x, TILE - 1, 0) for x in line] for line in t]
        new = []
        for i in range(ntile):
            mid = sides(t[i], lanes)
            line = []
            for j in range(nt):
                above = jnp.where(sub == 0, back[i - 1][j], back[i][j])
                below = jnp.where(sub == TILE - 1, fore[(i + 1) % ntile][j], fore[i][j])
                line.append((q[i][j] + (mid[j] + (above + below))) * rec[i][j])
            new.append(line)
        t = new
    for i in range(1, ntile - 1):
        for j in range(nt - 1):
            at = (slice((i - 1) * TILE, i * TILE), slice(j * LANES, (j + 1) * LANES))
            diss[at] = q[i][j]
            heat[at] = t[i][j]


def on_device(current_pattern, conductivity, cooling, harm_order, harm_amp, block_counts):
    slab, total = current_pattern.shape
    harm, mesh = lax.axis_size("harm"), lax.axis_size("mesh")
    width = total // harm
    wide = width + LANES
    chips = harm // 2
    held = -(-harm // TILE) * TILE
    any_space = pl.BlockSpec(memory_space=pl.ANY)
    vmem = pl.BlockSpec(memory_space=pltpu.VMEM)
    smem = pl.BlockSpec(memory_space=pltpu.SMEM)
    shape = lambda *s: jax.ShapeDtypeStruct(s, F32)
    fields = (current_pattern, conductivity, cooling)

    own, other, params = pl.pallas_call(
        functools.partial(pack_kernel, width=width),
        out_shape=(shape(2 * TILE, wide), shape(2 * TILE, wide), shape(held, LANES)),
        in_specs=[smem] * 3 + [any_space] * 3,
        out_specs=(vmem,) * 3,
        scratch_shapes=[
            pltpu.VMEM((3, TILE, min(2 * width + 2 * LANES, total)), F32),
            pltpu.SemaphoreType.DMA((3,)),
        ],
        name="pack",
    )(harm_order, harm_amp, block_counts, *fields)

    axes = ("mesh", "harm")

    def permute(value, target):
        pairs = []
        for m in range(mesh):
            for z in range(chips):
                for c in range(2):
                    tm, tz, tc = target(m, z, c)
                    pairs.append(
                        (m * harm + z * 2 + c, (tm % mesh) * harm + (tz % chips) * 2 + tc)
                    )
        return lax.ppermute(value, axes, pairs)

    def swap(value):
        return permute(value, lambda m, z, c: (m, z, 1 - c))

    def beside(m, z, c):
        return m + (1 - 2 * c), z, c

    got = permute(own, beside)
    pass_on = permute(other, beside)
    params = jnp.maximum(params, swap(params))
    steps = list(range(1, chips))
    if len(steps) % 2:
        steps.append(1)
    power = chips & (chips - 1) == 0
    known = params
    for a, b in zip(steps[::2], steps[1::2]):
        def hop(m, z, c, a=a, b=b):
            k = (a, b)[c]
            return m, (z ^ k if power else z + k), c
        known = jnp.maximum(known, permute(params, hop))
    known_too = swap(known)
    passed = swap(pass_on)

    tile_cur, tile_con, tile_coo = pl.pallas_call(
        functools.partial(gather_kernel, width=width),
        out_shape=(shape(slab, wide),) * 3,
        in_specs=[any_space] * 3,
        out_specs=(vmem,) * 3,
        scratch_shapes=[
            pltpu.VMEM((3, slab, min(width + 2 * LANES, total)), F32),
            pltpu.SemaphoreType.DMA((3,)),
        ],
        name="gather",
    )(*fields)

    ext = slab + 2 * TILE
    flat = pltpu.VMEM((ext, wide), F32)
    deep = pltpu.VMEM((ext, TILE, wide), F32)
    return pl.pallas_call(
        functools.partial(loss_kernel, width=width, harmonics=harm),
        out_shape=(shape(slab, width),) * 2,
        in_specs=[vmem] * 7,
        out_specs=(vmem,) * 2,
        scratch_shapes=[flat] * 3 + [deep] * 7 + [flat],
        compiler_params=pltpu.CompilerParams(vmem_limit_bytes=24 * 2**20),
        name="losses",
    )(known, known_too, tile_cur, tile_con, tile_coo, got, passed)


def solution(mesh):
    return jax.shard_map(
        on_device,
        mesh=mesh,
        in_specs=(P("mesh", None),) * 3 + (P("harm"),) * 3,
        out_specs=(P("mesh", "harm"), P("mesh", "harm")),
        check_vma=False,
    )
```

```python
import functools

import jax
import jax.numpy as jnp
from jax import lax
from jax.experimental import pallas as pl
from jax.experimental.pallas import tpu as pltpu
from jax.sharding import PartitionSpec as P

LANES = 128
HALF = 64
TILE = 8
BASE_FREQ = 0.1
MARGIN = 5
F32 = jnp.float32


def lane_iota(rows=TILE):
    return lax.broadcasted_iota(jnp.int32, (rows, LANES), 1)


def sublane_iota():
    return lax.broadcasted_iota(jnp.int32, (TILE, LANES), 0)


def side_tile(buf, rows, left, right):
    lanes = lane_iota(rows.size if hasattr(rows, "size") else rows.stop - rows.start)
    after = buf[rows, pl.ds(pl.multiple_of(right, LANES), LANES)]
    before = buf[rows, pl.ds(pl.multiple_of(left, LANES), LANES)]
    return jnp.where(lanes < HALF, after, before)


def window(start, size, total):
    begin = jnp.clip(start - LANES, 0, total - size)
    return pl.multiple_of(begin, LANES)


def params_kernel(order, amp, count, params):
    h = lax.axis_index("harm")
    rows = lax.broadcasted_iota(jnp.int32, params.shape, 0)
    lanes = lax.broadcasted_iota(jnp.int32, params.shape, 1)
    value = jnp.where(
        lanes == 0, order[0], jnp.where(lanes == 1, amp[0], count[0])
    ).astype(F32)
    params[...] = jnp.where((rows == h) & (lanes < 3), value, 0.0)


def pack_kernel(after, cur, con, coo, out, cur_out, con_out, coo_out, buf, held, sems, *, width):
    slab, total = cur.shape
    h = lax.axis_index("harm")
    core = lax.rem(h, 2)
    size = buf.shape[2]
    first = (h - core) * width
    begin = window(first, size, total)
    row = pl.multiple_of(jnp.where(core == 0, slab - TILE, 0), TILE)
    copies = [
        pltpu.make_async_copy(
            ref.at[pl.ds(row, TILE), pl.ds(begin, size)], buf.at[i], sems.at[i]
        )
        for i, ref in enumerate((cur, con, coo))
    ]
    for copy in copies:
        copy.start()
    size_own = held.shape[2]
    begin_own = window(h * width, size_own, total)
    own = [
        pltpu.make_async_copy(
            ref.at[:, pl.ds(begin_own, size_own)], held.at[i], sems.at[3 + i]
        )
        for i, ref in enumerate((cur, con, coo))
    ]
    for copy in own:
        copy.start()
    sub = sublane_iota()
    goes_up = core == 0
    shift = jnp.where(goes_up, 3, 5)
    take_cur = jnp.where(goes_up, sub - 3, 4 - sub) >= 0
    for copy in copies:
        copy.wait()
    for part, target in enumerate((core, 1 - core)):
        offset = first + target * width - begin
        left = jnp.maximum(offset - LANES, 0)
        right = jnp.minimum(offset + width, size - LANES)
        pieces = []
        for j in range(width // LANES):
            at = pl.ds(pl.multiple_of(offset + j * LANES, LANES), LANES)
            pieces.append([buf[i, :, at] for i in range(3)])
        pieces.append(
            [side_tile(buf.at[i], slice(0, TILE), left, right) for i in range(3)]
        )
        base = part * 2 * TILE
        for j, (a, b, c) in enumerate(pieces):
            at = slice(j * LANES, (j + 1) * LANES)
            out[base : base + TILE, at] = jnp.where(take_cur, a, pltpu.roll(c, shift, 0))
            out[base + TILE : base + 2 * TILE, at] = b
    offset = h * width - begin_own
    left = jnp.maximum(offset - LANES, 0)
    right = jnp.minimum(offset + width, size_own - LANES)
    for i, tile in enumerate((cur_out, con_out, coo_out)):
        own[i].wait()
        tile[:, :width] = held[i, :, pl.ds(pl.multiple_of(offset, LANES), width)]
        tile[:, width:] = side_tile(held.at[i], slice(0, slab), left, right)


def pass_kernel(after, got, passed):
    passed[...] = got[2 * TILE :, :]


def sides(tiles, lanes):
    n = len(tiles)
    back = [pltpu.roll(t, 1, 1) for t in tiles]
    fore = [pltpu.roll(t, LANES - 1, 1) for t in tiles]
    return [
        jnp.where(lanes == 0, back[j - 1], back[j])
        + jnp.where(lanes == LANES - 1, fore[(j + 1) % n], fore[j])
        for j in range(n)
    ]


def fold_harmonics(rows, sub):
    level = list(rows)
    for half in (4, 2, 1):
        low = (sub & half) == 0
        merged = []
        for i in range(half):
            a, b = level[i], level[i + half]
            if a is None and b is None:
                merged.append(None)
                continue
            a = jnp.zeros((TILE, LANES), F32) if a is None else a
            b = jnp.zeros((TILE, LANES), F32) if b is None else b
            keep = jnp.where(low, a, b)
            move = jnp.where(low, b, a)
            merged.append(keep + jnp.where(low, pltpu.roll(move, TILE - half, 0), pltpu.roll(move, half, 0)))
        level = merged
    return level[0]


def loss_kernel(
    par_ref, cur, con, coo, near, far, diss, heat,
    xcur, xcon, xcoo, rr, gg, ss, ra, ha, rb, hb, qq, *, width, harmonics,
):
    slab = cur.shape[0]
    nt = width // LANES + 1
    top, bottom = TILE, TILE + slab
    ext = slab + 2 * TILE
    h = lax.axis_index("harm")
    m = lax.axis_index("mesh")
    last_h = lax.axis_size("harm") - 1
    last_m = lax.axis_size("mesh") - 1
    core = lax.rem(h, 2)
    lanes, sub = lane_iota(), sublane_iota()
    xcur[top:bottom, :] = cur[...]
    xcon[top:bottom, :] = con[...]
    xcoo[top:bottom, :] = coo[...]

    def edges(up, down):
        xcur[0:TILE, :] = up[:TILE, :]
        xcon[0:TILE, :] = up[TILE : 2 * TILE, :]
        xcoo[0:TILE, :] = pltpu.roll(up[:TILE, :], TILE - 3, 0)
        xcur[bottom:ext, :] = down[:TILE, :]
        xcon[bottom:ext, :] = down[TILE : 2 * TILE, :]
        xcoo[bottom:ext, :] = pltpu.roll(down[:TILE, :], TILE - 5, 0)

    @pl.when(core == 0)
    def _():
        edges(near, far)

    @pl.when(core == 1)
    def _():
        edges(far, near)

    has_up = (m > 0).astype(F32)
    has_down = (m < last_m).astype(F32)
    has_left = (h > 0).astype(F32)
    has_right = (h < last_h).astype(F32)
    col_tile = (h * (width // LANES)).astype(F32)
    zero = jnp.zeros((TILE, LANES), F32)

    for group in range((harmonics + TILE - 1) // TILE):
        at = slice(group * TILE, (group + 1) * TILE)
        par = par_ref[at, :]
        order = jnp.broadcast_to(par[:, 0:1], (TILE, LANES))
        amp = jnp.broadcast_to(par[:, 1:2], (TILE, LANES))
        count = jnp.broadcast_to(par[:, 2:3], (TILE, LANES))
        omega = BASE_FREQ * order
        quarter = 0.25 * omega
        weight = (0.5 / harmonics) * omega * amp * amp
        masks = [
            jnp.where(count > col_tile + j, 0.25, 0.0) for j in range(nt - 1)
        ]
        masks.append(
            jnp.where(
                lanes < HALF,
                jnp.where(count > col_tile + (nt - 1), 0.25 * has_right, 0.0),
                jnp.where(count > col_tile - 1, 0.25 * has_left, 0.0),
            )
        )

        def start_rows(base, subs, scale):
            scaled = masks if scale is None else [k * scale for k in masks]
            for j in range(nt):
                col = slice(j * LANES, (j + 1) * LANES)
                a = xcur[pl.ds(base, TILE), col]
                b = xcon[pl.ds(base, TILE), col]
                for s in subs:
                    src = jnp.broadcast_to(a[s : s + 1, :], (TILE, LANES))
                    g = quarter * jnp.broadcast_to(b[s : s + 1, :], (TILE, LANES))
                    d = 1.0 + g * g
                    r = pl.reciprocal(d, approx=True)
                    r = r * (2.0 - d * r)
                    r = r * scaled[j]
                    re = src * r
                    rr[base + s, :, col] = r
                    gg[base + s, :, col] = g
                    ss[base + s, :, col] = src
                    ra[base + s, :, col] = re
                    ha[base + s, :, col] = g * re

        start_rows(0, range(TILE - MARGIN, TILE), has_up)
        start_rows(bottom, range(MARGIN), has_down)

        def start_body(i, carry):
            start_rows(pl.multiple_of(top + i * TILE, TILE), range(TILE), None)
            return carry

        lax.fori_loop(0, slab // TILE, start_body, 0)

        def load(ref, row):
            return [ref[row, :, j * LANES : (j + 1) * LANES] for j in range(nt)]

        def near_sum(ref, row):
            mid = sides(load(ref, row), lanes)
            return [
                x + (u + v)
                for x, u, v in zip(mid, load(ref, row - 1), load(ref, row + 1))
            ]

        def sweep_rows(base, subs):
            for s in subs:
                row = base + s
                nr, nh = near_sum(ra, row), near_sum(ha, row)
                r, g, src = load(rr, row), load(gg, row), load(ss, row)
                for j in range(nt):
                    col = slice(j * LANES, (j + 1) * LANES)
                    x = src[j] + nr[j]
                    rb[row, :, col] = r[j] * (x - g[j] * nh[j])
                    hb[row, :, col] = r[j] * (g[j] * x + nh[j])

        def sweep_body(i, carry):
            sweep_rows(TILE - MARGIN + 1 + i * TILE, range(TILE))
            return carry

        lax.fori_loop(0, (slab + 2 * (MARGIN - 1)) // TILE, sweep_body, 0)

        def loss_rows(base, subs):
            rows = [[None] * TILE for _ in range(nt)]
            for s in subs:
                row = base + s
                nr, nh = near_sum(rb, row), near_sum(hb, row)
                r, g, src = load(rr, row), load(gg, row), load(ss, row)
                for j in range(nt):
                    x = src[j] + nr[j]
                    rows[j][s] = (weight * g[j] * r[j]) * (x * x + nh[j] * nh[j])
            for j in range(nt):
                col = slice(j * LANES, (j + 1) * LANES)
                total = fold_harmonics(rows[j], sub)
                if group:
                    total = qq[pl.ds(base, TILE), col] + total
                qq[pl.ds(base, TILE), col] = total

        loss_rows(0, range(TILE - MARGIN + 2, TILE))
        loss_rows(bottom, range(MARGIN - 2))

        def loss_body(i, carry):
            loss_rows(pl.multiple_of(top + i * TILE, TILE), range(TILE))
            return carry

        lax.fori_loop(0, slab // TILE, loss_body, 0)

    ntile = ext // TILE
    side = jnp.where(lanes < HALF, has_right, has_left)
    q = [[qq[i * TILE : (i + 1) * TILE, j * LANES : (j + 1) * LANES] for j in range(nt)] for i in range(ntile)]
    rec = []
    for i in range(ntile):
        line = []
        for j in range(nt):
            w = 1.0 / (4.0 + xcoo[i * TILE : (i + 1) * TILE, j * LANES : (j + 1) * LANES])
            if i == 0:
                w = w * has_up
            if i == ntile - 1:
                w = w * has_down
            if j == nt - 1:
                w = w * side
            line.append(w)
        rec.append(line)
    t = [[q[i][j] * rec[i][j] for j in range(nt)] for i in range(ntile)]
    for _ in range(3):
        back = [[pltpu.roll(x, 1, 0) for x in line] for line in t]
        fore = [[pltpu.roll(x, TILE - 1, 0) for x in line] for line in t]
        new = []
        for i in range(ntile):
            mid = sides(t[i], lanes)
            line = []
            for j in range(nt):
                above = jnp.where(sub == 0, back[i - 1][j], back[i][j])
                below = jnp.where(sub == TILE - 1, fore[(i + 1) % ntile][j], fore[i][j])
                line.append((q[i][j] + (mid[j] + (above + below))) * rec[i][j])
            new.append(line)
        t = new
    for i in range(1, ntile - 1):
        for j in range(nt - 1):
            at = (slice((i - 1) * TILE, i * TILE), slice(j * LANES, (j + 1) * LANES))
            diss[at] = q[i][j]
            heat[at] = t[i][j]


def on_device(current_pattern, conductivity, cooling, harm_order, harm_amp, block_counts):
    slab, total = current_pattern.shape
    harm, mesh = lax.axis_size("harm"), lax.axis_size("mesh")
    width = total // harm
    wide = width + LANES
    chips = harm // 2
    held = -(-harm // TILE) * TILE
    any_space = pl.BlockSpec(memory_space=pl.ANY)
    vmem = pl.BlockSpec(memory_space=pltpu.VMEM)
    smem = pl.BlockSpec(memory_space=pltpu.SMEM)
    shape = lambda *s: jax.ShapeDtypeStruct(s, F32)
    fields = (current_pattern, conductivity, cooling)

    small = pltpu.CompilerParams(vmem_limit_bytes=4 * 2**20)
    in_hbm = lambda x: pltpu.with_memory_space_constraint(x, pltpu.HBM)
    held_vmem = lambda *s: pltpu.VMEM(s, F32)
    params = pl.pallas_call(
        params_kernel,
        out_shape=held_vmem(held, LANES),
        in_specs=[smem] * 3,
        out_specs=vmem,
        compiler_params=small,
        name="params",
    )(harm_order, harm_amp, block_counts)
    edges, tile_cur, tile_con, tile_coo = pl.pallas_call(
        functools.partial(pack_kernel, width=width),
        out_shape=(held_vmem(4 * TILE, wide),) + (held_vmem(slab, wide),) * 3,
        in_specs=[any_space] * 4,
        out_specs=(vmem,) * 4,
        scratch_shapes=[
            pltpu.VMEM((3, TILE, min(2 * width + 2 * LANES, total)), F32),
            pltpu.VMEM((3, slab, min(width + 2 * LANES, total)), F32),
            pltpu.SemaphoreType.DMA((6,)),
        ],
        compiler_params=small,
        name="pack",
    )(params, *map(in_hbm, fields))

    axes = ("mesh", "harm")

    def permute(value, target):
        pairs = []
        for m in range(mesh):
            for z in range(chips):
                for c in range(2):
                    tm, tz, tc = target(m, z, c)
                    pairs.append(
                        (m * harm + z * 2 + c, (tm % mesh) * harm + (tz % chips) * 2 + tc)
                    )
        return lax.ppermute(value, axes, pairs)

    def swap(value):
        return permute(value, lambda m, z, c: (m, z, 1 - c))

    def beside(m, z, c):
        return m + (1 - 2 * c), z, c

    known = jnp.maximum(params, swap(params))
    stages = [known]
    edges, known = lax.optimization_barrier((edges, known))
    got = permute(edges, beside)
    if chips & (chips - 1) == 0:
        step = 1
        while step < chips:
            known = jnp.maximum(
                known, permute(known, lambda m, z, c: (m, z ^ step, c))
            )
            stages.append(known)
            step *= 2
    else:
        table = known
        for step in range(1, chips):
            known = jnp.maximum(
                known, permute(table, lambda m, z, c: (m, z + step, c))
            )
            stages.append(known)
    passed = pl.pallas_call(
        pass_kernel,
        out_shape=held_vmem(2 * TILE, wide),
        in_specs=[any_space, vmem],
        out_specs=vmem,
        compiler_params=small,
        name="pass_on",
    )(stages[min(1, len(stages) - 1)], got)
    far = swap(passed)

    ext = slab + 2 * TILE
    flat = pltpu.VMEM((ext, wide), F32)
    deep = pltpu.VMEM((ext, TILE, wide), F32)
    return pl.pallas_call(
        functools.partial(loss_kernel, width=width, harmonics=harm),
        out_shape=(shape(slab, width),) * 2,
        in_specs=[vmem] * 6,
        out_specs=(vmem,) * 2,
        scratch_shapes=[flat] * 3 + [deep] * 7 + [flat],
        compiler_params=pltpu.CompilerParams(vmem_limit_bytes=12 * 2**20),
        name="losses",
    )(known, tile_cur, tile_con, tile_coo, got, far)


def solution(mesh):
    return jax.shard_map(
        on_device,
        mesh=mesh,
        in_specs=(P("mesh", None),) * 3 + (P("harm"),) * 3,
        out_specs=(P("mesh", "harm"), P("mesh", "harm")),
        check_vma=False,
    )
```

```python
import functools

import jax
import jax.numpy as jnp
from jax import lax
from jax.experimental import pallas as pl
from jax.experimental.pallas import tpu as pltpu
from jax.sharding import PartitionSpec as P

LANES = 128
HALF = 64
TILE = 8
BASE_FREQ = 0.1
MARGIN = 5
F32 = jnp.float32


def lane_iota(rows=TILE):
    return lax.broadcasted_iota(jnp.int32, (rows, LANES), 1)


def sublane_iota():
    return lax.broadcasted_iota(jnp.int32, (TILE, LANES), 0)


def side_tile(buf, rows, left, right):
    lanes = lane_iota(rows.size if hasattr(rows, "size") else rows.stop - rows.start)
    after = buf[rows, pl.ds(pl.multiple_of(right, LANES), LANES)]
    before = buf[rows, pl.ds(pl.multiple_of(left, LANES), LANES)]
    return jnp.where(lanes < HALF, after, before)


def window(start, size, total):
    begin = jnp.clip(start - LANES, 0, total - size)
    return pl.multiple_of(begin, LANES)


def params_kernel(order, amp, count, params):
    h = lax.axis_index("harm")
    rows = lax.broadcasted_iota(jnp.int32, params.shape, 0)
    lanes = lax.broadcasted_iota(jnp.int32, params.shape, 1)
    value = jnp.where(
        lanes == 0, order[0], jnp.where(lanes == 1, amp[0], count[0])
    ).astype(F32)
    params[...] = jnp.where((rows == h) & (lanes < 3), value, 0.0)


def pack_kernel(after, cur, con, coo, out, cur_out, con_out, coo_out, buf, held, sems, *, width):
    slab, total = cur.shape
    h = lax.axis_index("harm")
    core = lax.rem(h, 2)
    size = buf.shape[2]
    first = (h - core) * width
    begin = window(first, size, total)
    row = pl.multiple_of(jnp.where(core == 0, slab - TILE, 0), TILE)
    copies = [
        pltpu.make_async_copy(
            ref.at[pl.ds(row, TILE), pl.ds(begin, size)], buf.at[i], sems.at[i]
        )
        for i, ref in enumerate((cur, con, coo))
    ]
    for copy in copies:
        copy.start()
    size_own = held.shape[2]
    begin_own = window(h * width, size_own, total)
    own = [
        pltpu.make_async_copy(
            ref.at[:, pl.ds(begin_own, size_own)], held.at[i], sems.at[3 + i]
        )
        for i, ref in enumerate((cur, con, coo))
    ]
    for copy in own:
        copy.start()
    sub = sublane_iota()
    goes_up = core == 0
    shift = jnp.where(goes_up, 3, 5)
    take_cur = jnp.where(goes_up, sub - 3, 4 - sub) >= 0
    for copy in copies:
        copy.wait()
    for part, target in enumerate((core, 1 - core)):
        offset = first + target * width - begin
        left = jnp.maximum(offset - LANES, 0)
        right = jnp.minimum(offset + width, size - LANES)
        pieces = []
        for j in range(width // LANES):
            at = pl.ds(pl.multiple_of(offset + j * LANES, LANES), LANES)
            pieces.append([buf[i, :, at] for i in range(3)])
        pieces.append(
            [side_tile(buf.at[i], slice(0, TILE), left, right) for i in range(3)]
        )
        base = part * 2 * TILE
        for j, (a, b, c) in enumerate(pieces):
            at = slice(j * LANES, (j + 1) * LANES)
            out[base : base + TILE, at] = jnp.where(take_cur, a, pltpu.roll(c, shift, 0))
            out[base + TILE : base + 2 * TILE, at] = b
    offset = h * width - begin_own
    left = jnp.maximum(offset - LANES, 0)
    right = jnp.minimum(offset + width, size_own - LANES)
    for i, tile in enumerate((cur_out, con_out, coo_out)):
        own[i].wait()
        tile[:, :width] = held[i, :, pl.ds(pl.multiple_of(offset, LANES), width)]
        tile[:, width:] = side_tile(held.at[i], slice(0, slab), left, right)


def pass_kernel(after, got, passed):
    passed[...] = got[2 * TILE :, :]


def sides(tiles, lanes):
    n = len(tiles)
    back = [pltpu.roll(t, 1, 1) for t in tiles]
    fore = [pltpu.roll(t, LANES - 1, 1) for t in tiles]
    return [
        jnp.where(lanes == 0, back[j - 1], back[j])
        + jnp.where(lanes == LANES - 1, fore[(j + 1) % n], fore[j])
        for j in range(n)
    ]


def fold_harmonics(rows, sub):
    level = list(rows)
    for half in (4, 2, 1):
        low = (sub & half) == 0
        merged = []
        for i in range(half):
            a, b = level[i], level[i + half]
            if a is None and b is None:
                merged.append(None)
                continue
            a = jnp.zeros((TILE, LANES), F32) if a is None else a
            b = jnp.zeros((TILE, LANES), F32) if b is None else b
            keep = jnp.where(low, a, b)
            move = jnp.where(low, b, a)
            merged.append(keep + jnp.where(low, pltpu.roll(move, TILE - half, 0), pltpu.roll(move, half, 0)))
        level = merged
    return level[0]


def loss_kernel(
    par_ref, cur, con, coo, near, far, diss, heat,
    xcur, xcon, xcoo, rr, gg, ss, ra, ha, rb, hb, qq, *, width, harmonics,
):
    slab = cur.shape[0]
    nt = width // LANES + 1
    top, bottom = TILE, TILE + slab
    ext = slab + 2 * TILE
    h = lax.axis_index("harm")
    m = lax.axis_index("mesh")
    last_h = lax.axis_size("harm") - 1
    last_m = lax.axis_size("mesh") - 1
    core = lax.rem(h, 2)
    lanes, sub = lane_iota(), sublane_iota()
    xcur[top:bottom, :] = cur[...]
    xcon[top:bottom, :] = con[...]
    xcoo[top:bottom, :] = coo[...]

    def edges(up, down):
        xcur[0:TILE, :] = up[:TILE, :]
        xcon[0:TILE, :] = up[TILE : 2 * TILE, :]
        xcoo[0:TILE, :] = pltpu.roll(up[:TILE, :], TILE - 3, 0)
        xcur[bottom:ext, :] = down[:TILE, :]
        xcon[bottom:ext, :] = down[TILE : 2 * TILE, :]
        xcoo[bottom:ext, :] = pltpu.roll(down[:TILE, :], TILE - 5, 0)

    @pl.when(core == 0)
    def _():
        edges(near, far)

    @pl.when(core == 1)
    def _():
        edges(far, near)

    has_up = (m > 0).astype(F32)
    has_down = (m < last_m).astype(F32)
    has_left = (h > 0).astype(F32)
    has_right = (h < last_h).astype(F32)
    col_tile = (h * (width // LANES)).astype(F32)
    zero = jnp.zeros((TILE, LANES), F32)

    for group in range((harmonics + TILE - 1) // TILE):
        at = slice(group * TILE, (group + 1) * TILE)
        par = par_ref[at, :]
        order = jnp.broadcast_to(par[:, 0:1], (TILE, LANES))
        amp = jnp.broadcast_to(par[:, 1:2], (TILE, LANES))
        count = jnp.broadcast_to(par[:, 2:3], (TILE, LANES))
        omega = BASE_FREQ * order
        quarter = 0.25 * omega
        weight = (0.5 / harmonics) * omega * amp * amp
        masks = [
            jnp.where(count > col_tile + j, 0.25, 0.0) for j in range(nt - 1)
        ]
        masks.append(
            jnp.where(
                lanes < HALF,
                jnp.where(count > col_tile + (nt - 1), 0.25 * has_right, 0.0),
                jnp.where(count > col_tile - 1, 0.25 * has_left, 0.0),
            )
        )

        def start_rows(base, subs, scale):
            scaled = masks if scale is None else [k * scale for k in masks]
            for j in range(nt):
                col = slice(j * LANES, (j + 1) * LANES)
                a = xcur[pl.ds(base, TILE), col]
                b = xcon[pl.ds(base, TILE), col]
                for s in subs:
                    src = jnp.broadcast_to(a[s : s + 1, :], (TILE, LANES))
                    g = quarter * jnp.broadcast_to(b[s : s + 1, :], (TILE, LANES))
                    d = 1.0 + g * g
                    r = pl.reciprocal(d, approx=True)
                    r = r * (2.0 - d * r)
                    r = r * scaled[j]
                    re = src * r
                    rr[base + s, :, col] = r
                    gg[base + s, :, col] = g
                    ss[base + s, :, col] = src
                    ra[base + s, :, col] = re
                    ha[base + s, :, col] = g * re

        start_rows(0, range(TILE - MARGIN, TILE), has_up)
        start_rows(bottom, range(MARGIN), has_down)

        def start_body(i, carry):
            start_rows(pl.multiple_of(top + i * TILE, TILE), range(TILE), None)
            return carry

        lax.fori_loop(0, slab // TILE, start_body, 0)

        def load(ref, row):
            return [ref[row, :, j * LANES : (j + 1) * LANES] for j in range(nt)]

        def near_sum(ref, row):
            mid = sides(load(ref, row), lanes)
            return [
                x + (u + v)
                for x, u, v in zip(mid, load(ref, row - 1), load(ref, row + 1))
            ]

        def sweep_rows(base, subs):
            for s in subs:
                row = base + s
                nr, nh = near_sum(ra, row), near_sum(ha, row)
                r, g, src = load(rr, row), load(gg, row), load(ss, row)
                for j in range(nt):
                    col = slice(j * LANES, (j + 1) * LANES)
                    x = src[j] + nr[j]
                    rb[row, :, col] = r[j] * (x - g[j] * nh[j])
                    hb[row, :, col] = r[j] * (g[j] * x + nh[j])

        def sweep_body(i, carry):
            sweep_rows(TILE - MARGIN + 1 + i * TILE, range(TILE))
            return carry

        lax.fori_loop(0, (slab + 2 * (MARGIN - 1)) // TILE, sweep_body, 0)

        def loss_rows(base, subs):
            rows = [[None] * TILE for _ in range(nt)]
            for s in subs:
                row = base + s
                nr, nh = near_sum(rb, row), near_sum(hb, row)
                r, g, src = load(rr, row), load(gg, row), load(ss, row)
                for j in range(nt):
                    x = src[j] + nr[j]
                    rows[j][s] = (weight * g[j] * r[j]) * (x * x + nh[j] * nh[j])
            for j in range(nt):
                col = slice(j * LANES, (j + 1) * LANES)
                total = fold_harmonics(rows[j], sub)
                if group:
                    total = qq[pl.ds(base, TILE), col] + total
                qq[pl.ds(base, TILE), col] = total

        loss_rows(0, range(TILE - MARGIN + 2, TILE))
        loss_rows(bottom, range(MARGIN - 2))

        def loss_body(i, carry):
            loss_rows(pl.multiple_of(top + i * TILE, TILE), range(TILE))
            return carry

        lax.fori_loop(0, slab // TILE, loss_body, 0)

    ntile = ext // TILE
    side = jnp.where(lanes < HALF, has_right, has_left)
    q = [[qq[i * TILE : (i + 1) * TILE, j * LANES : (j + 1) * LANES] for j in range(nt)] for i in range(ntile)]
    rec = []
    for i in range(ntile):
        line = []
        for j in range(nt):
            w = 1.0 / (4.0 + xcoo[i * TILE : (i + 1) * TILE, j * LANES : (j + 1) * LANES])
            if i == 0:
                w = w * has_up
            if i == ntile - 1:
                w = w * has_down
            if j == nt - 1:
                w = w * side
            line.append(w)
        rec.append(line)
    t = [[q[i][j] * rec[i][j] for j in range(nt)] for i in range(ntile)]
    for _ in range(3):
        back = [[pltpu.roll(x, 1, 0) for x in line] for line in t]
        fore = [[pltpu.roll(x, TILE - 1, 0) for x in line] for line in t]
        new = []
        for i in range(ntile):
            mid = sides(t[i], lanes)
            line = []
            for j in range(nt):
                above = jnp.where(sub == 0, back[i - 1][j], back[i][j])
                below = jnp.where(sub == TILE - 1, fore[(i + 1) % ntile][j], fore[i][j])
                line.append((q[i][j] + (mid[j] + (above + below))) * rec[i][j])
            new.append(line)
        t = new
    for i in range(1, ntile - 1):
        for j in range(nt - 1):
            at = (slice((i - 1) * TILE, i * TILE), slice(j * LANES, (j + 1) * LANES))
            diss[at] = q[i][j]
            heat[at] = t[i][j]


def on_device(current_pattern, conductivity, cooling, harm_order, harm_amp, block_counts):
    slab, total = current_pattern.shape
    harm, mesh = lax.axis_size("harm"), lax.axis_size("mesh")
    width = total // harm
    wide = width + LANES
    chips = harm // 2
    held = -(-harm // TILE) * TILE
    any_space = pl.BlockSpec(memory_space=pl.ANY)
    vmem = pl.BlockSpec(memory_space=pltpu.VMEM)
    smem = pl.BlockSpec(memory_space=pltpu.SMEM)
    shape = lambda *s: jax.ShapeDtypeStruct(s, F32)
    fields = (current_pattern, conductivity, cooling)

    small = pltpu.CompilerParams(vmem_limit_bytes=4 * 2**20)
    in_hbm = lambda x: pltpu.with_memory_space_constraint(x, pltpu.HBM)
    held_vmem = lambda *s: pltpu.VMEM(s, F32)
    params = pl.pallas_call(
        params_kernel,
        out_shape=held_vmem(held, LANES),
        in_specs=[smem] * 3,
        out_specs=vmem,
        compiler_params=small,
        name="params",
    )(harm_order, harm_amp, block_counts)
    edges, tile_cur, tile_con, tile_coo = pl.pallas_call(
        functools.partial(pack_kernel, width=width),
        out_shape=(held_vmem(4 * TILE, wide),) + (held_vmem(slab, wide),) * 3,
        in_specs=[any_space] * 4,
        out_specs=(vmem,) * 4,
        scratch_shapes=[
            pltpu.VMEM((3, TILE, min(2 * width + 2 * LANES, total)), F32),
            pltpu.VMEM((3, slab, min(width + 2 * LANES, total)), F32),
            pltpu.SemaphoreType.DMA((6,)),
        ],
        compiler_params=small,
        name="pack",
    )(params, *map(in_hbm, fields))

    axes = ("mesh", "harm")

    def permute(value, target):
        pairs = []
        for m in range(mesh):
            for z in range(chips):
                for c in range(2):
                    tm, tz, tc = target(m, z, c)
                    pairs.append(
                        (m * harm + z * 2 + c, (tm % mesh) * harm + (tz % chips) * 2 + tc)
                    )
        return lax.ppermute(value, axes, pairs)

    def swap(value):
        return permute(value, lambda m, z, c: (m, z, 1 - c))

    def beside(m, z, c):
        return m + (1 - 2 * c), z, c

    known = jnp.maximum(params, swap(params))
    stages = [known]
    edges, known = lax.optimization_barrier((edges, known))
    got = permute(edges, beside)
    if chips & (chips - 1) == 0:
        step = 1
        while step < chips:
            sent = jnp.tile(known, (1, 2)) if step > 1 else known
            known = jnp.maximum(
                known, permute(sent, lambda m, z, c: (m, z ^ step, c))[:, :LANES]
            )
            stages.append(known)
            step *= 2
    else:
        table = known
        for step in range(1, chips):
            known = jnp.maximum(
                known, permute(table, lambda m, z, c: (m, z + step, c))
            )
            stages.append(known)
    passed = pl.pallas_call(
        pass_kernel,
        out_shape=held_vmem(2 * TILE, wide),
        in_specs=[any_space, vmem],
        out_specs=vmem,
        compiler_params=small,
        name="pass_on",
    )(stages[min(1, len(stages) - 1)], got)
    far = swap(passed)

    ext = slab + 2 * TILE
    flat = pltpu.VMEM((ext, wide), F32)
    deep = pltpu.VMEM((ext, TILE, wide), F32)
    return pl.pallas_call(
        functools.partial(loss_kernel, width=width, harmonics=harm),
        out_shape=(shape(slab, width),) * 2,
        in_specs=[vmem] * 6,
        out_specs=(vmem,) * 2,
        scratch_shapes=[flat] * 3 + [deep] * 7 + [flat],
        compiler_params=pltpu.CompilerParams(vmem_limit_bytes=12 * 2**20),
        name="losses",
    )(known, tile_cur, tile_con, tile_coo, got, far)


def solution(mesh):
    return jax.shard_map(
        on_device,
        mesh=mesh,
        in_specs=(P("mesh", None),) * 3 + (P("harm"),) * 3,
        out_specs=(P("mesh", "harm"), P("mesh", "harm")),
        check_vma=False,
    )
```

```python
import functools

import jax
import jax.numpy as jnp
from jax import lax
from jax.experimental import pallas as pl
from jax.experimental.pallas import tpu as pltpu
from jax.sharding import PartitionSpec as P

LANES = 128
HALF = 64
TILE = 8
BASE_FREQ = 0.1
MARGIN = 5
F32 = jnp.float32


def lane_iota(rows=TILE):
    return lax.broadcasted_iota(jnp.int32, (rows, LANES), 1)


def sublane_iota():
    return lax.broadcasted_iota(jnp.int32, (TILE, LANES), 0)


def side_tile(buf, rows, left, right):
    lanes = lane_iota(rows.size if hasattr(rows, "size") else rows.stop - rows.start)
    after = buf[rows, pl.ds(pl.multiple_of(right, LANES), LANES)]
    before = buf[rows, pl.ds(pl.multiple_of(left, LANES), LANES)]
    return jnp.where(lanes < HALF, after, before)


def lane_gather(x, index):
    return jnp.take_along_axis(x, index, axis=1)


def interleave(tiles):
    n, lanes = len(tiles), lane_iota()
    out = []
    for p in range(n):
        column = n * lanes + p
        index = lax.rem(column, LANES)
        if n % 2:
            mixed = tiles[0]
            for t in range(1, n):
                mixed = jnp.where(lax.rem(lanes + t * LANES - p + n, n) == 0, tiles[t], mixed)
            out.append(lane_gather(mixed, index))
        else:
            mixed = lane_gather(tiles[0], index)
            for t in range(1, n):
                mixed = jnp.where(column // LANES == t, lane_gather(tiles[t], index), mixed)
            out.append(mixed)
    return out


def natural(tiles, count):
    n, lanes = len(tiles), lane_iota()
    if n % 2:
        inverse = pow(n, -1, LANES)
        moved = [
            lane_gather(x, lax.rem(inverse * (lanes - p + LANES), LANES))
            for p, x in enumerate(tiles)
        ]
    out = []
    for t in range(count):
        column = t * LANES + lanes
        part = lambda p: moved[p] if n % 2 else lane_gather(tiles[p], column // n)
        mixed = part(0)
        for p in range(1, n):
            mixed = jnp.where(lax.rem(column, n) == p, part(p), mixed)
        out.append(mixed)
    return out


def window(start, size, total):
    begin = jnp.clip(start - LANES, 0, total - size)
    return pl.multiple_of(begin, LANES)


def params_kernel(order, amp, count, params):
    h = lax.axis_index("harm")
    rows = lax.broadcasted_iota(jnp.int32, params.shape, 0)
    lanes = lax.broadcasted_iota(jnp.int32, params.shape, 1)
    value = jnp.where(
        lanes == 0, order[0], jnp.where(lanes == 1, amp[0], count[0])
    ).astype(F32)
    params[...] = jnp.where((rows == h) & (lanes < 3), value, 0.0)


def pack_kernel(after, cur, con, coo, out, buf, sems, *, width):
    slab, total = cur.shape
    h = lax.axis_index("harm")
    core = lax.rem(h, 2)
    size = buf.shape[2]
    first = (h - core) * width
    begin = window(first, size, total)
    row = pl.multiple_of(jnp.where(core == 0, slab - TILE, 0), TILE)
    copies = [
        pltpu.make_async_copy(
            ref.at[pl.ds(row, TILE), pl.ds(begin, size)], buf.at[i], sems.at[i]
        )
        for i, ref in enumerate((cur, con, coo))
    ]
    for copy in copies:
        copy.start()
    sub = sublane_iota()
    goes_up = core == 0
    shift = jnp.where(goes_up, 3, 5)
    take_cur = jnp.where(goes_up, sub - 3, 4 - sub) >= 0
    for copy in copies:
        copy.wait()
    for part, target in enumerate((core, 1 - core)):
        offset = first + target * width - begin
        left = jnp.maximum(offset - LANES, 0)
        right = jnp.minimum(offset + width, size - LANES)
        fields = []
        for i in range(3):
            tiles = [
                buf[i, :, pl.ds(pl.multiple_of(offset + j * LANES, LANES), LANES)]
                for j in range(width // LANES)
            ]
            tiles.append(side_tile(buf.at[i], slice(0, TILE), left, right))
            fields.append(interleave(tiles))
        base = part * 2 * TILE
        for j, (a, b, c) in enumerate(zip(*fields)):
            at = slice(j * LANES, (j + 1) * LANES)
            out[base : base + TILE, at] = jnp.where(take_cur, a, pltpu.roll(c, shift, 0))
            out[base + TILE : base + 2 * TILE, at] = b


def arrange_kernel(after, cur, con, coo, cur_out, con_out, coo_out, held, sems, *, width):
    slab, total = cur.shape
    h = lax.axis_index("harm")
    size = held.shape[2]
    begin = window(h * width, size, total)
    copies = [
        pltpu.make_async_copy(ref.at[:, pl.ds(begin, size)], held.at[i], sems.at[i])
        for i, ref in enumerate((cur, con, coo))
    ]
    for copy in copies:
        copy.start()
    offset = h * width - begin
    left = jnp.maximum(offset - LANES, 0)
    right = jnp.minimum(offset + width, size - LANES)
    for i, tile in enumerate((cur_out, con_out, coo_out)):
        copies[i].wait()
        for r in range(0, slab, TILE):
            rows = slice(r, r + TILE)
            pieces = [
                held[i, rows, pl.ds(pl.multiple_of(offset + j * LANES, LANES), LANES)]
                for j in range(width // LANES)
            ]
            pieces.append(side_tile(held.at[i], rows, left, right))
            for j, piece in enumerate(interleave(pieces)):
                tile[rows, j * LANES : (j + 1) * LANES] = piece


def pass_kernel(after, got, passed):
    passed[...] = got[2 * TILE :, :]


def sides(tiles):
    line = [pltpu.roll(tiles[-1], 1, 1), *tiles, pltpu.roll(tiles[0], LANES - 1, 1)]
    return [a + b for a, b in zip(line[:-2], line[2:])]


class Fold:
    def __init__(self, sub):
        self.low = [(sub & shift) == 0 for shift in (1, 2, 4)]
        self.held = [None] * 3

    def add(self, value):
        for level in range(3):
            first, self.held[level] = self.held[level], None
            if first is None:
                self.held[level] = value
                return None
            low = self.low[level]
            value = jnp.where(low, first, value) + pltpu.roll(
                jnp.where(low, value, first), 1 << level, 0
            )
        return value


def loss_kernel(
    par_ref, cur, con, coo, near, far, diss, heat,
    xcur, xcon, xcoo, rr, gg, ss, ra, ha, rb, hb, qq, results, sems, *, width, harmonics,
):
    slab = cur.shape[0]
    nt = width // LANES + 1
    top, bottom = TILE, TILE + slab
    ext = slab + 2 * TILE
    h = lax.axis_index("harm")
    m = lax.axis_index("mesh")
    last_h = lax.axis_size("harm") - 1
    last_m = lax.axis_size("mesh") - 1
    core = lax.rem(h, 2)
    lanes, sub = lane_iota(), sublane_iota()
    xcur[top:bottom, :] = cur[...]
    xcon[top:bottom, :] = con[...]
    xcoo[top:bottom, :] = coo[...]

    def edges(up, down):
        xcur[0:TILE, :] = up[:TILE, :]
        xcon[0:TILE, :] = up[TILE : 2 * TILE, :]
        xcoo[0:TILE, :] = pltpu.roll(up[:TILE, :], TILE - 3, 0)
        xcur[bottom:ext, :] = down[:TILE, :]
        xcon[bottom:ext, :] = down[TILE : 2 * TILE, :]
        xcoo[bottom:ext, :] = pltpu.roll(down[:TILE, :], TILE - 5, 0)

    @pl.when(core == 0)
    def _():
        edges(near, far)

    @pl.when(core == 1)
    def _():
        edges(far, near)

    has_up = (m > 0).astype(F32)
    has_down = (m < last_m).astype(F32)
    has_left = (h > 0).astype(F32)
    has_right = (h < last_h).astype(F32)
    columns = [nt * lanes + j for j in range(nt)]
    inside = [
        jnp.where(c < width, 1.0, jnp.where(c < width + HALF, has_right, has_left))
        for c in columns
    ]

    def first_block(j):
        block = jnp.where(columns[j] < width + HALF, columns[j] // LANES, -1)
        return (block + h * (width // LANES)).astype(F32)


    for group in range((harmonics + TILE - 1) // TILE):
        at = slice(group * TILE, (group + 1) * TILE)
        par = par_ref[at, :]
        order = jnp.broadcast_to(par[:, 0:1], (TILE, LANES))
        amp = jnp.broadcast_to(par[:, 1:2], (TILE, LANES))
        count = jnp.broadcast_to(par[:, 2:3], (TILE, LANES))
        omega = BASE_FREQ * order
        quarter = 0.25 * omega
        weight = (0.5 / harmonics) * omega * amp * amp
        masks = [
            jnp.where(count > first_block(j), 0.25 * inside[j], 0.0) for j in range(nt)
        ]

        def start_rows(base, subs, scale):
            scaled = masks if scale is None else [k * scale for k in masks]
            for j in range(nt):
                col = slice(j * LANES, (j + 1) * LANES)
                a = xcur[pl.ds(base, TILE), col]
                b = xcon[pl.ds(base, TILE), col]
                for s in subs:
                    src = jnp.broadcast_to(a[s : s + 1, :], (TILE, LANES))
                    g = quarter * jnp.broadcast_to(b[s : s + 1, :], (TILE, LANES))
                    d = 1.0 + g * g
                    r = pl.reciprocal(d, approx=True)
                    r = r * (2.0 - d * r)
                    r = r * scaled[j]
                    re = src * r
                    rr[base + s, :, col] = r
                    gg[base + s, :, col] = g
                    ss[base + s, :, col] = src
                    ra[base + s, :, col] = re
                    ha[base + s, :, col] = g * re

        start_rows(0, range(TILE - MARGIN, TILE), has_up)
        start_rows(bottom, range(MARGIN), has_down)

        def start_body(i, carry):
            start_rows(pl.multiple_of(top + i * TILE, TILE), range(TILE), None)
            return carry

        lax.fori_loop(0, slab // TILE, start_body, 0, unroll=True)

        def load(ref, row):
            return [ref[row, :, j * LANES : (j + 1) * LANES] for j in range(nt)]

        def cached(ref):
            rows = {}

            def get(base, s):
                if s not in rows:
                    rows[s] = load(ref, base + s)
                return rows[s]

            return get

        def near_sum(get, base, s):
            mid = sides(get(base, s))
            return [
                x + (u + v)
                for x, u, v in zip(mid, get(base, s - 1), get(base, s + 1))
            ]

        def sweep_rows(base, subs):
            get_r, get_h = cached(ra), cached(ha)
            for s in subs:
                row = base + s
                nr, nh = near_sum(get_r, base, s), near_sum(get_h, base, s)
                r, g, src = load(rr, row), load(gg, row), load(ss, row)
                for j in range(nt):
                    col = slice(j * LANES, (j + 1) * LANES)
                    x = src[j] + nr[j]
                    rb[row, :, col] = r[j] * (x - g[j] * nh[j])
                    hb[row, :, col] = r[j] * (g[j] * x + nh[j])

        def sweep_body(i, carry):
            sweep_rows(TILE - MARGIN + 1 + i * TILE, range(TILE))
            return carry

        lax.fori_loop(0, (slab + 2 * (MARGIN - 1)) // TILE, sweep_body, 0, unroll=True)

        def loss_rows(base, subs):
            folds, totals = [Fold(sub) for _ in range(nt)], [None] * nt
            zero = jnp.zeros((TILE, LANES), F32)
            get_r, get_h = cached(rb), cached(hb)
            for s in range(TILE):
                if s not in subs:
                    totals = [fold.add(zero) for fold in folds]
                    continue
                row = base + s
                nr, nh = near_sum(get_r, base, s), near_sum(get_h, base, s)
                r, g, src = load(rr, row), load(gg, row), load(ss, row)
                for j in range(nt):
                    x = src[j] + nr[j]
                    totals[j] = folds[j].add(
                        (weight * g[j] * r[j]) * (x * x + nh[j] * nh[j])
                    )
            for j in range(nt):
                col = slice(j * LANES, (j + 1) * LANES)
                total = totals[j]
                if group:
                    total = qq[pl.ds(base, TILE), col] + total
                qq[pl.ds(base, TILE), col] = total

        loss_rows(0, range(TILE - MARGIN + 2, TILE))
        loss_rows(bottom, range(MARGIN - 2))

        def loss_body(i, carry):
            loss_rows(pl.multiple_of(top + i * TILE, TILE), range(TILE))
            return carry

        lax.fori_loop(0, slab // TILE, loss_body, 0, unroll=True)

    ntile = ext // TILE
    q = [[qq[i * TILE : (i + 1) * TILE, j * LANES : (j + 1) * LANES] for j in range(nt)] for i in range(ntile)]

    def hand_out(k, lines):
        for i in range(1, ntile - 1):
            for j, tile in enumerate(natural(lines[i], nt - 1)):
                results[k, (i - 1) * TILE : i * TILE, j * LANES : (j + 1) * LANES] = tile
        copy = pltpu.make_async_copy(results.at[k], (diss, heat)[k], sems.at[k])
        copy.start()
        return copy

    first = hand_out(0, q)
    rec = []
    for i in range(ntile):
        line = []
        for j in range(nt):
            w = 1.0 / (4.0 + xcoo[i * TILE : (i + 1) * TILE, j * LANES : (j + 1) * LANES])
            if i == 0:
                w = w * has_up
            if i == ntile - 1:
                w = w * has_down
            line.append(w * inside[j])
        rec.append(line)
    t = [[q[i][j] * rec[i][j] for j in range(nt)] for i in range(ntile)]
    for _ in range(3):
        back = [[pltpu.roll(x, 1, 0) for x in line] for line in t]
        fore = [[pltpu.roll(x, TILE - 1, 0) for x in line] for line in t]
        new = []
        for i in range(ntile):
            mid = sides(t[i])
            line = []
            for j in range(nt):
                above = jnp.where(sub == 0, back[i - 1][j], back[i][j])
                below = jnp.where(sub == TILE - 1, fore[(i + 1) % ntile][j], fore[i][j])
                line.append((q[i][j] + (mid[j] + (above + below))) * rec[i][j])
            new.append(line)
        t = new
    second = hand_out(1, t)
    first.wait()
    second.wait()


def on_device(current_pattern, conductivity, cooling, harm_order, harm_amp, block_counts):
    slab, total = current_pattern.shape
    harm, mesh = lax.axis_size("harm"), lax.axis_size("mesh")
    width = total // harm
    wide = width + LANES
    chips = harm // 2
    held = -(-harm // TILE) * TILE
    any_space = pl.BlockSpec(memory_space=pl.ANY)
    vmem = pl.BlockSpec(memory_space=pltpu.VMEM)
    smem = pl.BlockSpec(memory_space=pltpu.SMEM)
    shape = lambda *s: jax.ShapeDtypeStruct(s, F32)
    fields = (current_pattern, conductivity, cooling)

    small = pltpu.CompilerParams(vmem_limit_bytes=4 * 2**20)
    in_hbm = lambda x: pltpu.with_memory_space_constraint(x, pltpu.HBM)
    held_vmem = lambda *s: pltpu.VMEM(s, F32)
    params = pl.pallas_call(
        params_kernel,
        out_shape=held_vmem(held, LANES),
        in_specs=[smem] * 3,
        out_specs=vmem,
        compiler_params=small,
        name="params",
    )(harm_order, harm_amp, block_counts)
    edges = pl.pallas_call(
        functools.partial(pack_kernel, width=width),
        out_shape=held_vmem(4 * TILE, wide),
        in_specs=[any_space] * 4,
        out_specs=vmem,
        scratch_shapes=[
            pltpu.VMEM((3, TILE, min(2 * width + 2 * LANES, total)), F32),
            pltpu.SemaphoreType.DMA((3,)),
        ],
        compiler_params=small,
        name="pack",
    )(params, *map(in_hbm, fields))
    axes = ("mesh", "harm")

    def permute(value, target):
        pairs = []
        for m in range(mesh):
            for z in range(chips):
                for c in range(2):
                    tm, tz, tc = target(m, z, c)
                    pairs.append(
                        (m * harm + z * 2 + c, (tm % mesh) * harm + (tz % chips) * 2 + tc)
                    )
        return lax.ppermute(value, axes, pairs)

    def swap(value):
        return permute(value, lambda m, z, c: (m, z, 1 - c))

    def beside(m, z, c):
        return m + (1 - 2 * c), z, c

    known = jnp.maximum(params, swap(params))
    edges, before = lax.optimization_barrier((edges, known))
    got = permute(edges, beside)
    power = chips & (chips - 1) == 0
    steps = [1 << i for i in range(chips.bit_length() - 1)] if power else range(1, chips)
    last = table = before
    for i, step in enumerate(steps):
        before = jnp.maximum(before, last)
        if power:
            table = before
        sent = jnp.tile(table, (1, 2)) if i else table
        hop = lambda m, z, c: (m, z ^ step if power else z + step, c)
        last = permute(sent, hop)[:, :LANES]
    passed = pl.pallas_call(
        pass_kernel,
        out_shape=held_vmem(2 * TILE, wide),
        in_specs=[any_space, vmem],
        out_specs=vmem,
        compiler_params=small,
        name="pass_on",
    )(before, got)
    far = swap(passed)

    tile_cur, tile_con, tile_coo = pl.pallas_call(
        functools.partial(arrange_kernel, width=width),
        out_shape=(held_vmem(slab, wide),) * 3,
        in_specs=[any_space] * 4,
        out_specs=(vmem,) * 3,
        scratch_shapes=[
            pltpu.VMEM((3, slab, min(width + 2 * LANES, total)), F32),
            pltpu.SemaphoreType.DMA((3,)),
        ],
        compiler_params=small,
        name="arrange",
    )(passed, *fields)

    before, tile_cur = lax.optimization_barrier((before, tile_cur))
    known = jnp.maximum(before, last)
    ext = slab + 2 * TILE
    flat = pltpu.VMEM((ext, wide), F32)
    deep = pltpu.VMEM((ext, TILE, wide), F32)
    return pl.pallas_call(
        functools.partial(loss_kernel, width=width, harmonics=harm),
        out_shape=(shape(slab, width),) * 2,
        in_specs=[vmem] * 6,
        out_specs=(any_space,) * 2,
        scratch_shapes=[flat] * 3
        + [deep] * 7
        + [flat, pltpu.VMEM((2, slab, width), F32), pltpu.SemaphoreType.DMA((2,))],
        compiler_params=pltpu.CompilerParams(vmem_limit_bytes=12 * 2**20),
        name="losses",
    )(known, tile_cur, tile_con, tile_coo, got, far)


def solution(mesh):
    return jax.shard_map(
        on_device,
        mesh=mesh,
        in_specs=(P("mesh", None),) * 3 + (P("harm"),) * 3,
        out_specs=(P("mesh", "harm"), P("mesh", "harm")),
        check_vma=False,
    )
```

```python
import functools

import jax
import jax.numpy as jnp
from jax import lax
from jax.experimental import pallas as pl
from jax.experimental.pallas import tpu as pltpu
from jax.sharding import PartitionSpec as P

LANES = 128
HALF = 64
TILE = 8
BASE_FREQ = 0.1
MARGIN = 5
F32 = jnp.float32


def lane_iota(rows=TILE):
    return lax.broadcasted_iota(jnp.int32, (rows, LANES), 1)


def sublane_iota():
    return lax.broadcasted_iota(jnp.int32, (TILE, LANES), 0)


def side_tile(buf, rows, left, right):
    lanes = lane_iota(rows.size if hasattr(rows, "size") else rows.stop - rows.start)
    after = buf[rows, pl.ds(pl.multiple_of(right, LANES), LANES)]
    before = buf[rows, pl.ds(pl.multiple_of(left, LANES), LANES)]
    return jnp.where(lanes < HALF, after, before)


def lane_gather(x, index):
    return jnp.take_along_axis(x, index, axis=1)


class Columns:
    def __init__(self, n):
        self.n, lanes = n, lane_iota()
        self.columns = [n * lanes + p for p in range(n)]
        if n % 2:
            inverse = pow(n, -1, LANES)
            self.index = [lax.rem(c, LANES) for c in self.columns]
            self.back = [lax.rem(inverse * (lanes - p + LANES), LANES) for p in range(n)]
            phase = lax.rem(lanes, n)
            self.phase = [phase == k for k in range(n)]
        else:
            self.index = [lax.rem(c, LANES) for c in self.columns]
            self.back = [(t * LANES + lanes) // n for t in range(n)]

    def interleave(self, tiles):
        n, out = self.n, []
        for p in range(n):
            if n % 2:
                mixed = tiles[0]
                for t in range(1, n):
                    mixed = jnp.where(self.phase[(p - t * LANES) % n], tiles[t], mixed)
                out.append(lane_gather(mixed, self.index[p]))
            else:
                mixed = lane_gather(tiles[0], self.index[p])
                for t in range(1, n):
                    mixed = jnp.where(
                        self.columns[p] // LANES == t,
                        lane_gather(tiles[t], self.index[p]),
                        mixed,
                    )
                out.append(mixed)
        return out

    def natural(self, tiles, count):
        n, out = self.n, []
        if n % 2:
            tiles = [lane_gather(x, self.back[p]) for p, x in enumerate(tiles)]
        for t in range(count):
            if n % 2:
                mixed = tiles[0]
                for p in range(1, n):
                    mixed = jnp.where(self.phase[(p - t * LANES) % n], tiles[p], mixed)
            else:
                lanes = lane_iota()
                mixed = lane_gather(tiles[0], self.back[t])
                for p in range(1, n):
                    mixed = jnp.where(
                        lax.rem(lanes, n) == p, lane_gather(tiles[p], self.back[t]), mixed
                    )
            out.append(mixed)
        return out


def window(start, size, total):
    begin = jnp.clip(start - LANES, 0, total - size)
    return pl.multiple_of(begin, LANES)


def params_kernel(order, amp, count, params):
    h = lax.axis_index("harm")
    rows = lax.broadcasted_iota(jnp.int32, params.shape, 0)
    lanes = lax.broadcasted_iota(jnp.int32, params.shape, 1)
    value = jnp.where(
        lanes == 0, order[0], jnp.where(lanes == 1, amp[0], count[0])
    ).astype(F32)
    params[...] = jnp.where((rows == h) & (lanes < 3), value, 0.0)


def pack_kernel(after, cur, con, coo, out, buf, sems, *, width):
    slab, total = cur.shape
    h = lax.axis_index("harm")
    core = lax.rem(h, 2)
    size = buf.shape[2]
    first = (h - core) * width
    begin = window(first, size, total)
    row = pl.multiple_of(jnp.where(core == 0, slab - TILE, 0), TILE)
    copies = [
        pltpu.make_async_copy(
            ref.at[pl.ds(row, TILE), pl.ds(begin, size)], buf.at[i], sems.at[i]
        )
        for i, ref in enumerate((cur, con, coo))
    ]
    for copy in copies:
        copy.start()
    columns = Columns(width // LANES + 1)
    sub = sublane_iota()
    goes_up = core == 0
    shift = jnp.where(goes_up, 3, 5)
    take_cur = jnp.where(goes_up, sub - 3, 4 - sub) >= 0
    for copy in copies:
        copy.wait()
    for part, target in enumerate((core, 1 - core)):
        offset = first + target * width - begin
        left = jnp.maximum(offset - LANES, 0)
        right = jnp.minimum(offset + width, size - LANES)
        fields = []
        for i in range(3):
            tiles = [
                buf[i, :, pl.ds(pl.multiple_of(offset + j * LANES, LANES), LANES)]
                for j in range(width // LANES)
            ]
            tiles.append(side_tile(buf.at[i], slice(0, TILE), left, right))
            fields.append(columns.interleave(tiles))
        base = part * 2 * TILE
        for j, (a, b, c) in enumerate(zip(*fields)):
            at = slice(j * LANES, (j + 1) * LANES)
            out[base : base + TILE, at] = jnp.where(take_cur, a, pltpu.roll(c, shift, 0))
            out[base + TILE : base + 2 * TILE, at] = b


def arrange_kernel(after, cur, con, coo, cur_out, con_out, coo_out, held, sems, *, width):
    slab, total = cur.shape
    h = lax.axis_index("harm")
    size = held.shape[2]
    begin = window(h * width, size, total)
    copies = [
        pltpu.make_async_copy(ref.at[:, pl.ds(begin, size)], held.at[i], sems.at[i])
        for i, ref in enumerate((cur, con, coo))
    ]
    for copy in copies:
        copy.start()
    offset = h * width - begin
    left = jnp.maximum(offset - LANES, 0)
    right = jnp.minimum(offset + width, size - LANES)
    columns = Columns(width // LANES + 1)
    for i, tile in enumerate((cur_out, con_out, coo_out)):
        copies[i].wait()
        for r in range(0, slab, TILE):
            rows = slice(r, r + TILE)
            pieces = [
                held[i, rows, pl.ds(pl.multiple_of(offset + j * LANES, LANES), LANES)]
                for j in range(width // LANES)
            ]
            pieces.append(side_tile(held.at[i], rows, left, right))
            for j, piece in enumerate(columns.interleave(pieces)):
                tile[rows, j * LANES : (j + 1) * LANES] = piece


def pass_kernel(after, got, passed):
    passed[...] = got[2 * TILE :, :]


def sides(tiles):
    line = [pltpu.roll(tiles[-1], 1, 1), *tiles, pltpu.roll(tiles[0], LANES - 1, 1)]
    return [a + b for a, b in zip(line[:-2], line[2:])]


class Fold:
    def __init__(self, sub):
        self.low = [(sub & shift) == 0 for shift in (1, 2, 4)]
        self.held = [None] * 3

    def add(self, value):
        for level in range(3):
            first, self.held[level] = self.held[level], None
            if first is None:
                self.held[level] = value
                return None
            low = self.low[level]
            value = jnp.where(low, first, value) + pltpu.roll(
                jnp.where(low, value, first), 1 << level, 0
            )
        return value


def loss_kernel(
    par_ref, cur, con, coo, near, far, diss, heat,
    xcur, xcon, xcoo, rr, rb, hb, qq, results, sems, *, width, harmonics,
):
    slab = cur.shape[0]
    nt = width // LANES + 1
    top, bottom = TILE, TILE + slab
    ext = slab + 2 * TILE
    h = lax.axis_index("harm")
    m = lax.axis_index("mesh")
    last_h = lax.axis_size("harm") - 1
    last_m = lax.axis_size("mesh") - 1
    core = lax.rem(h, 2)
    lanes, sub = lane_iota(), sublane_iota()
    cols = [slice(j * LANES, (j + 1) * LANES) for j in range(nt)]
    xcur[top:bottom, :] = cur[...]
    xcon[top:bottom, :] = con[...]
    xcoo[top:bottom, :] = coo[...]

    def edges(up, down):
        xcur[0:TILE, :] = up[:TILE, :]
        xcon[0:TILE, :] = up[TILE : 2 * TILE, :]
        xcoo[0:TILE, :] = pltpu.roll(up[:TILE, :], TILE - 3, 0)
        xcur[bottom:ext, :] = down[:TILE, :]
        xcon[bottom:ext, :] = down[TILE : 2 * TILE, :]
        xcoo[bottom:ext, :] = pltpu.roll(down[:TILE, :], TILE - 5, 0)

    @pl.when(core == 0)
    def _():
        edges(near, far)

    @pl.when(core == 1)
    def _():
        edges(far, near)

    has_up = (m > 0).astype(F32)
    has_down = (m < last_m).astype(F32)
    has_left = (h > 0).astype(F32)
    has_right = (h < last_h).astype(F32)
    order_of = Columns(nt)
    columns = order_of.columns
    inside = [
        jnp.where(c < width, 1.0, jnp.where(c < width + HALF, has_right, has_left))
        for c in columns
    ]

    def first_block(j):
        block = jnp.where(columns[j] < width + HALF, columns[j] // LANES, -1)
        return (block + h * (width // LANES)).astype(F32)


    ntile = ext // TILE
    losses, weights, levels, copies = [], [], [[], [], [], []], []

    def hand_out(k, i, tiles):
        rows = slice((i - 1) * TILE, i * TILE)
        for col, tile in zip(cols, order_of.natural(tiles, nt - 1)):
            results[k, rows, col] = tile
        copy = pltpu.make_async_copy(
            results.at[k, rows, :], (diss, heat)[k].at[rows, :], sems.at[k, i - 1]
        )
        copy.start()
        copies.append(copy)

    def sweep(i, before):
        rolled = lambda k, shift: [pltpu.roll(x, shift, 0) for x in before[k]]
        above, below = rolled(i, 1), rolled(i, TILE - 1)
        if i > 0:
            above = [jnp.where(sub == 0, p, x) for p, x in zip(rolled(i - 1, 1), above)]
        if i < ntile - 1:
            below = [jnp.where(sub == TILE - 1, p, x) for p, x in zip(rolled(i + 1, TILE - 1), below)]
        return [
            (q + (x + (a + b))) * w
            for q, x, a, b, w in zip(losses[i], sides(before[i]), above, below, weights[i])
        ]

    def conduct(i, q):
        losses.append(q)
        scale = has_up if i == 0 else has_down if i == ntile - 1 else None
        w = [
            pl.reciprocal(4.0 + xcoo[i * TILE : (i + 1) * TILE, col], approx=True) * x
            for col, x in zip(cols, inside)
        ]
        weights.append(w if scale is None else [x * scale for x in w])
        levels[0].append([a * b for a, b in zip(q, weights[i])])
        if 0 < i < ntile - 1:
            hand_out(0, i, q)
        for k in range(1, 4):
            ready = [i - k] if i < ntile - 1 else list(range(max(i - k, 0), ntile))
            for at in ready:
                if at >= 0:
                    outer = at in (0, ntile - 1)
                    levels[k].append(None if k == 3 and outer else sweep(at, levels[k - 1]))
                    if k == 3 and not outer:
                        hand_out(1, at, levels[3][at])

    groups = (harmonics + TILE - 1) // TILE
    for group in range(groups):
        at = slice(group * TILE, (group + 1) * TILE)
        par = par_ref[at, :]
        order = jnp.broadcast_to(par[:, 0:1], (TILE, LANES))
        amp = jnp.broadcast_to(par[:, 1:2], (TILE, LANES))
        count = jnp.broadcast_to(par[:, 2:3], (TILE, LANES))
        omega = BASE_FREQ * order
        quarter = 0.25 * omega
        scale_of_loss = (0.5 / harmonics) * quarter * omega * amp * amp
        zero = jnp.zeros((TILE, LANES), F32)
        masks = [
            jnp.where(count > first_block(j), 0.25 * inside[j], 0.0) for j in range(nt)
        ]

        def spread(ref, row):
            return [
                jnp.broadcast_to(ref[row : row + 1, j * LANES : (j + 1) * LANES], (TILE, LANES))
                for j in range(nt)
            ]

        def load(ref, row):
            return [ref[row, :, j * LANES : (j + 1) * LANES] for j in range(nt)]

        def store(ref, row, tiles):
            for j, tile in enumerate(tiles):
                ref[row, :, j * LANES : (j + 1) * LANES] = tile

        def pair(here, below):
            below = [*below[1:], pltpu.roll(below[0], LANES - 1, 1)]
            return [a + b for a, b in zip(here, below)]

        def neighbours(above, here):
            here = [pltpu.roll(here[-1], 1, 1), *here[:-1]]
            return [a + b for a, b in zip(above, here)]

        def slope(row):
            return [quarter * x for x in spread(xcon, row)]

        first, last = top - MARGIN, bottom + MARGIN - 1
        up = [k * has_up for k in masks]
        down = [k * has_down for k in masks]
        old = old_pairs = None
        for row in range(first, last + 1):
            scale = up if row < top else down if row >= bottom else masks
            src, g = spread(xcur, row), slope(row)
            r = [
                pl.reciprocal(1.0 + x * x, approx=True) * k for x, k in zip(g, scale)
            ]
            re = [a * b for a, b in zip(src, r)]
            him = [a * b for a, b in zip(g, re)]
            if first + 2 <= row <= last - 2:
                store(rr, row, r)
            if old is not None:
                pairs = pair(old[0], re), pair(old[1], him)
                if old_pairs is not None:
                    nr = neighbours(old_pairs[0], pairs[0])
                    nh = neighbours(old_pairs[1], pairs[1])
                    x = [a + b for a, b in zip(old[4], nr)]
                    store(rb, row - 1, [k * (a - b * c) for k, a, b, c in zip(old[2], x, old[3], nh)])
                    store(hb, row - 1, [k * (b * a + c) for k, a, b, c in zip(old[2], x, old[3], nh)])
                old_pairs = pairs
            old = re, him, r, g, src

        old = old_pairs = None
        folds, totals = [Fold(sub) for _ in range(nt)], None
        for row in range(ext):
            if first + 1 <= row + 1 <= last - 1 and old is None:
                old = load(rb, row + 1), load(hb, row + 1)
            elif old is not None and row + 1 <= last - 1:
                new = load(rb, row + 1), load(hb, row + 1)
                pairs = pair(old[0], new[0]), pair(old[1], new[1])
                old = new
                if old_pairs is not None:
                    nr = neighbours(old_pairs[0], pairs[0])
                    nh = neighbours(old_pairs[1], pairs[1])
                    src, con_row, r = spread(xcur, row), spread(xcon, row), load(rr, row)
                    for j in range(nt):
                        x = src[j] + nr[j]
                        loss = (scale_of_loss * con_row[j] * r[j]) * (x * x + nh[j] * nh[j])
                        totals = (totals or []) + [folds[j].add(loss)]
                old_pairs = pairs
            if totals is None:
                totals = [fold.add(zero) for fold in folds]
            if row % TILE == TILE - 1:
                i = row // TILE
                rows = slice(i * TILE, (i + 1) * TILE)
                if group:
                    totals = [qq[rows, col] + total for col, total in zip(cols, totals)]
                if group < groups - 1:
                    for col, total in zip(cols, totals):
                        qq[rows, col] = total
                else:
                    conduct(i, totals)
            totals = None

    for copy in copies:
        copy.wait()


def on_device(current_pattern, conductivity, cooling, harm_order, harm_amp, block_counts):
    slab, total = current_pattern.shape
    harm, mesh = lax.axis_size("harm"), lax.axis_size("mesh")
    width = total // harm
    wide = width + LANES
    chips = harm // 2
    held = -(-harm // TILE) * TILE
    any_space = pl.BlockSpec(memory_space=pl.ANY)
    vmem = pl.BlockSpec(memory_space=pltpu.VMEM)
    smem = pl.BlockSpec(memory_space=pltpu.SMEM)
    shape = lambda *s: jax.ShapeDtypeStruct(s, F32)
    fields = (current_pattern, conductivity, cooling)

    small = pltpu.CompilerParams(vmem_limit_bytes=4 * 2**20)
    in_hbm = lambda x: pltpu.with_memory_space_constraint(x, pltpu.HBM)
    held_vmem = lambda *s: pltpu.VMEM(s, F32)
    params = pl.pallas_call(
        params_kernel,
        out_shape=held_vmem(held, LANES),
        in_specs=[smem] * 3,
        out_specs=vmem,
        compiler_params=small,
        name="params",
    )(harm_order, harm_amp, block_counts)
    edges = pl.pallas_call(
        functools.partial(pack_kernel, width=width),
        out_shape=held_vmem(4 * TILE, wide),
        in_specs=[any_space] * 4,
        out_specs=vmem,
        scratch_shapes=[
            pltpu.VMEM((3, TILE, min(2 * width + 2 * LANES, total)), F32),
            pltpu.SemaphoreType.DMA((3,)),
        ],
        compiler_params=small,
        name="pack",
    )(params, *map(in_hbm, fields))
    axes = ("mesh", "harm")

    def permute(value, target):
        pairs = []
        for m in range(mesh):
            for z in range(chips):
                for c in range(2):
                    tm, tz, tc = target(m, z, c)
                    pairs.append(
                        (m * harm + z * 2 + c, (tm % mesh) * harm + (tz % chips) * 2 + tc)
                    )
        return lax.ppermute(value, axes, pairs)

    def swap(value):
        return permute(value, lambda m, z, c: (m, z, 1 - c))

    def beside(m, z, c):
        if m == (0 if c else mesh - 1):
            return m, z, 1 - c
        return m + (1 - 2 * c), z, c

    known = jnp.maximum(params, swap(params))
    edges, before = lax.optimization_barrier((edges, known))
    got = permute(edges, beside)
    power = chips & (chips - 1) == 0
    steps = [1 << i for i in range(chips.bit_length() - 1)] if power else range(1, chips)
    last = table = before
    for i, step in enumerate(steps):
        before = jnp.maximum(before, last)
        if power:
            table = before
        sent = jnp.tile(table, (1, 2)) if i else table
        hop = lambda m, z, c: (m, z ^ step if power else z + step, c)
        last = permute(sent, hop)[:, :LANES]
    passed = pl.pallas_call(
        pass_kernel,
        out_shape=held_vmem(2 * TILE, wide),
        in_specs=[any_space, vmem],
        out_specs=vmem,
        compiler_params=small,
        name="pass_on",
    )(before, got)
    far = swap(passed)

    tile_cur, tile_con, tile_coo = pl.pallas_call(
        functools.partial(arrange_kernel, width=width),
        out_shape=(held_vmem(slab, wide),) * 3,
        in_specs=[any_space] * 4,
        out_specs=(vmem,) * 3,
        scratch_shapes=[
            pltpu.VMEM((3, slab, min(width + 2 * LANES, total)), F32),
            pltpu.SemaphoreType.DMA((3,)),
        ],
        compiler_params=small,
        name="arrange",
    )(passed, *fields)

    before, tile_cur = lax.optimization_barrier((before, tile_cur))
    known = jnp.maximum(before, last)
    ext = slab + 2 * TILE
    flat = pltpu.VMEM((ext, wide), F32)
    deep = pltpu.VMEM((ext, TILE, wide), F32)
    return pl.pallas_call(
        functools.partial(loss_kernel, width=width, harmonics=harm),
        out_shape=(shape(slab, width),) * 2,
        in_specs=[vmem] * 6,
        out_specs=(any_space,) * 2,
        scratch_shapes=[flat] * 3
        + [deep] * 3
        + [flat, pltpu.VMEM((2, slab, width), F32), pltpu.SemaphoreType.DMA((2, slab // TILE))],
        compiler_params=pltpu.CompilerParams(vmem_limit_bytes=12 * 2**20),
        name="losses",
    )(known, tile_cur, tile_con, tile_coo, got, far)


def solution(mesh):
    return jax.shard_map(
        on_device,
        mesh=mesh,
        in_specs=(P("mesh", None),) * 3 + (P("harm"),) * 3,
        out_specs=(P("mesh", "harm"), P("mesh", "harm")),
        check_vma=False,
    )
```

```python
import functools

import jax
import jax.numpy as jnp
from jax import lax
from jax.experimental import pallas as pl
from jax.experimental.pallas import tpu as pltpu
from jax.sharding import PartitionSpec as P

LANES = 128
HALF = 64
TILE = 8
BASE_FREQ = 0.1
MARGIN = 5
F32 = jnp.float32


def lane_iota(rows=TILE):
    return lax.broadcasted_iota(jnp.int32, (rows, LANES), 1)


def sublane_iota():
    return lax.broadcasted_iota(jnp.int32, (TILE, LANES), 0)


def side_tile(buf, rows, left, right):
    lanes = lane_iota(rows.size if hasattr(rows, "size") else rows.stop - rows.start)
    after = buf[rows, pl.ds(pl.multiple_of(right, LANES), LANES)]
    before = buf[rows, pl.ds(pl.multiple_of(left, LANES), LANES)]
    return jnp.where(lanes < HALF, after, before)


def lane_gather(x, index):
    return jnp.take_along_axis(x, index, axis=1)


class Columns:
    def __init__(self, n):
        self.n, lanes = n, lane_iota()
        self.columns = [n * lanes + p for p in range(n)]
        if n % 2:
            inverse = pow(n, -1, LANES)
            self.index = [lax.rem(c, LANES) for c in self.columns]
            self.back = [lax.rem(inverse * (lanes - p + LANES), LANES) for p in range(n)]
            phase = lax.rem(lanes, n)
            self.phase = [phase == k for k in range(n)]
        else:
            self.index = [lax.rem(c, LANES) for c in self.columns]
            self.back = [(t * LANES + lanes) // n for t in range(n)]

    def interleave(self, tiles):
        n, out = self.n, []
        for p in range(n):
            if n % 2:
                mixed = tiles[0]
                for t in range(1, n):
                    mixed = jnp.where(self.phase[(p - t * LANES) % n], tiles[t], mixed)
                out.append(lane_gather(mixed, self.index[p]))
            else:
                mixed = lane_gather(tiles[0], self.index[p])
                for t in range(1, n):
                    mixed = jnp.where(
                        self.columns[p] // LANES == t,
                        lane_gather(tiles[t], self.index[p]),
                        mixed,
                    )
                out.append(mixed)
        return out

    def natural(self, tiles, count):
        n, out = self.n, []
        if n % 2:
            tiles = [lane_gather(x, self.back[p]) for p, x in enumerate(tiles)]
        for t in range(count):
            if n % 2:
                mixed = tiles[0]
                for p in range(1, n):
                    mixed = jnp.where(self.phase[(p - t * LANES) % n], tiles[p], mixed)
            else:
                lanes = lane_iota()
                mixed = lane_gather(tiles[0], self.back[t])
                for p in range(1, n):
                    mixed = jnp.where(
                        lax.rem(lanes, n) == p, lane_gather(tiles[p], self.back[t]), mixed
                    )
            out.append(mixed)
        return out


def window(start, size, total):
    begin = jnp.clip(start - LANES, 0, total - size)
    return pl.multiple_of(begin, LANES)


def params_kernel(order, amp, count, params):
    h = lax.axis_index("harm")
    rows = lax.broadcasted_iota(jnp.int32, params.shape, 0)
    lanes = lax.broadcasted_iota(jnp.int32, params.shape, 1)
    value = jnp.where(
        lanes == 0, order[0], jnp.where(lanes == 1, amp[0], count[0])
    ).astype(F32)
    params[...] = jnp.where((rows == h) & (lanes < 3), value, 0.0)


def pack_kernel(after, cur, con, coo, out, buf, sems, *, width):
    slab, total = cur.shape
    h = lax.axis_index("harm")
    core = lax.rem(h, 2)
    size = buf.shape[2]
    first = (h - core) * width
    begin = window(first, size, total)
    row = pl.multiple_of(jnp.where(core == 0, slab - TILE, 0), TILE)
    copies = [
        pltpu.make_async_copy(
            ref.at[pl.ds(row, TILE), pl.ds(begin, size)], buf.at[i], sems.at[i]
        )
        for i, ref in enumerate((cur, con, coo))
    ]
    for copy in copies:
        copy.start()
    columns = Columns(width // LANES + 1)
    sub = sublane_iota()
    goes_up = core == 0
    shift = jnp.where(goes_up, 3, 5)
    take_cur = jnp.where(goes_up, sub - 3, 4 - sub) >= 0
    for copy in copies:
        copy.wait()
    for part, target in enumerate((core, 1 - core)):
        offset = first + target * width - begin
        left = jnp.maximum(offset - LANES, 0)
        right = jnp.minimum(offset + width, size - LANES)
        fields = []
        for i in range(3):
            tiles = [
                buf[i, :, pl.ds(pl.multiple_of(offset + j * LANES, LANES), LANES)]
                for j in range(width // LANES)
            ]
            tiles.append(side_tile(buf.at[i], slice(0, TILE), left, right))
            fields.append(tiles)
        joined = [
            jnp.where(take_cur, a, pltpu.roll(c, shift, 0))
            for a, c in zip(fields[0], fields[2])
        ]
        for i, tiles in enumerate((joined, fields[1])):
            rows = slice((2 * part + i) * TILE, (2 * part + i + 1) * TILE)
            for j, tile in enumerate(columns.interleave(tiles)):
                out[rows, j * LANES : (j + 1) * LANES] = tile


def arrange_kernel(after, cur, con, coo, cur_out, con_out, coo_out, held, sems, *, width):
    slab, total = cur.shape
    h = lax.axis_index("harm")
    size = held.shape[2]
    begin = window(h * width, size, total)
    copies = [
        pltpu.make_async_copy(ref.at[:, pl.ds(begin, size)], held.at[i], sems.at[i])
        for i, ref in enumerate((cur, con, coo))
    ]
    for copy in copies:
        copy.start()
    offset = h * width - begin
    left = jnp.maximum(offset - LANES, 0)
    right = jnp.minimum(offset + width, size - LANES)
    columns = Columns(width // LANES + 1)
    for i, tile in enumerate((cur_out, con_out, coo_out)):
        copies[i].wait()
        for r in range(0, slab, TILE):
            rows = slice(r, r + TILE)
            pieces = [
                held[i, rows, pl.ds(pl.multiple_of(offset + j * LANES, LANES), LANES)]
                for j in range(width // LANES)
            ]
            pieces.append(side_tile(held.at[i], rows, left, right))
            for j, piece in enumerate(columns.interleave(pieces)):
                tile[rows, j * LANES : (j + 1) * LANES] = piece


def pass_kernel(after, got, passed):
    passed[...] = got[2 * TILE :, :]


def sides(tiles):
    line = [pltpu.roll(tiles[-1], 1, 1), *tiles, pltpu.roll(tiles[0], LANES - 1, 1)]
    return [a + b for a, b in zip(line[:-2], line[2:])]


class Fold:
    def __init__(self, sub):
        self.low = [(sub & shift) == 0 for shift in (1, 2, 4)]
        self.held = [None] * 3

    def add(self, value):
        for level in range(3):
            first, self.held[level] = self.held[level], None
            if first is None:
                self.held[level] = value
                return None
            low = self.low[level]
            value = jnp.where(low, first, value) + pltpu.roll(
                jnp.where(low, value, first), 1 << level, 0
            )
        return value


def load(ref, row, nt):
    return [ref[row, :, j * LANES : (j + 1) * LANES] for j in range(nt)]


def store(ref, row, tiles):
    for j, tile in enumerate(tiles):
        ref[row, :, j * LANES : (j + 1) * LANES] = tile


def spread(ref, row, nt):
    return [
        jnp.broadcast_to(ref[row : row + 1, j * LANES : (j + 1) * LANES], (TILE, LANES))
        for j in range(nt)
    ]


def pair(here, below):
    below = [*below[1:], pltpu.roll(below[0], LANES - 1, 1)]
    return [a + b for a, b in zip(here, below)]


def neighbours(above, here):
    here = [pltpu.roll(here[-1], 1, 1), *here[:-1]]
    return [a + b for a, b in zip(above, here)]


class Place:
    def __init__(self, width):
        self.width, self.nt = width, width // LANES + 1
        self.h, m = lax.axis_index("harm"), lax.axis_index("mesh")
        self.has_up = (m > 0).astype(F32)
        self.has_down = (m < lax.axis_size("mesh") - 1).astype(F32)
        has_left = (self.h > 0).astype(F32)
        has_right = (self.h < lax.axis_size("harm") - 1).astype(F32)
        self.order_of = Columns(self.nt)
        self.inside = [
            jnp.where(c < width, 1.0, jnp.where(c < width + HALF, has_right, has_left))
            for c in self.order_of.columns
        ]

    def first_block(self, j):
        c = self.order_of.columns[j]
        block = jnp.where(c < self.width + HALF, c // LANES, -1)
        return (block + self.h * (self.width // LANES)).astype(F32)

    def edges(self, near, far, put):
        core = lax.rem(self.h, 2)

        @pl.when(core == 0)
        def _():
            put(near, far)

        @pl.when(core == 1)
        def _():
            put(far, near)


def eddy(place, par, harmonics, start, count_rows, source, conductivity, valid, rr, rb, hb, loss_out):
    nt = place.nt
    order, amp, count = [
        jnp.broadcast_to(par[:, k : k + 1], (TILE, LANES)) for k in range(3)
    ]
    omega = BASE_FREQ * order
    quarter = 0.25 * omega
    scale_of_loss = (0.5 / harmonics) * quarter * omega * amp * amp
    masks = [
        jnp.where(count > place.first_block(j), 0.25 * place.inside[j], 0.0)
        for j in range(nt)
    ]
    scaled = {None: masks}

    old = old_pairs = None
    if start:
        zeros = [jnp.zeros((TILE, LANES), F32)] * nt
        store(rb, start - 1, zeros)
        store(hb, start - 1, zeros)
        old = zeros, zeros
    for row in range(start, count_rows):
        name, factor = valid(row)
        if name not in scaled:
            scaled[name] = [k * factor for k in masks]
        src = source(row)
        g = [quarter * x for x in conductivity(row)]
        r = [
            pl.reciprocal(1.0 + x * x, approx=True) * k for x, k in zip(g, scaled[name])
        ]
        re = [a * b for a, b in zip(src, r)]
        him = [a * b for a, b in zip(g, re)]
        if 2 <= row < count_rows - 2:
            store(rr, row, r)
        if old is not None:
            pairs = pair(old[0], re), pair(old[1], him)
            if old_pairs is not None:
                nr = neighbours(old_pairs[0], pairs[0])
                nh = neighbours(old_pairs[1], pairs[1])
                x = [a + b for a, b in zip(old[4], nr)]
                store(rb, row - 1, [k * (a - b * c) for k, a, b, c in zip(old[2], x, old[3], nh)])
                store(hb, row - 1, [k * (b * a + c) for k, a, b, c in zip(old[2], x, old[3], nh)])
            old_pairs = pairs
        old = re, him, r, g, src

    begin = max(start - 1, 1)
    old, old_pairs = (load(rb, begin, nt), load(hb, begin, nt)), None
    for row in range(begin, count_rows - 2):
        new = load(rb, row + 1, nt), load(hb, row + 1, nt)
        pairs = pair(old[0], new[0]), pair(old[1], new[1])
        old = new
        if old_pairs is not None:
            nr = neighbours(old_pairs[0], pairs[0])
            nh = neighbours(old_pairs[1], pairs[1])
            src, con, r = source(row), conductivity(row), load(rr, row, nt)
            losses = []
            for j in range(nt):
                x = src[j] + nr[j]
                losses.append(
                    (scale_of_loss * con[j] * r[j]) * (x * x + nh[j] * nh[j])
                )
            loss_out(row, losses)
        old_pairs = pairs


def loss_kernel(
    table, cur, con, coo, near, far, diss, heat,
    xcur, xcon, xcoo, rr, rb, hb, qq, results, sems, *, width, harmonics,
):
    slab = coo.shape[0]
    top, bottom = TILE, TILE + slab
    ext = slab + 2 * TILE
    place, nt, sub = Place(width), width // LANES + 1, sublane_iota()
    cols = [slice(j * LANES, (j + 1) * LANES) for j in range(nt)]
    xcur[top:bottom, :] = cur[...]
    xcon[top:bottom, :] = con[...]
    xcoo[top:bottom, :] = coo[...]

    def put(up, down):
        xcur[0:TILE, :] = up[:TILE, :]
        xcon[0:TILE, :] = up[TILE : 2 * TILE, :]
        xcoo[0:TILE, :] = jnp.maximum(pltpu.roll(up[:TILE, :], TILE - 3, 0), 0.0)
        xcur[bottom:ext, :] = down[:TILE, :]
        xcon[bottom:ext, :] = down[TILE : 2 * TILE, :]
        xcoo[bottom:ext, :] = jnp.maximum(pltpu.roll(down[:TILE, :], TILE - 5, 0), 0.0)

    place.edges(near, far, put)

    def run(start):
        ntile = ext // TILE
        losses, weights, levels, copies = [], [], [[], [], [], []], []
        if start:
            nothing = [jnp.zeros((TILE, LANES), F32)] * nt
            losses.append(nothing)
            weights.append(nothing)
            for level in levels:
                level.append(nothing)

        def hand_out(k, i, tiles):
            rows = slice((i - 1) * TILE, i * TILE)
            for col, tile in zip(cols, place.order_of.natural(tiles, nt - 1)):
                results[k, rows, col] = tile
            copy = pltpu.make_async_copy(
                results.at[k, rows, :], (diss, heat)[k].at[rows, :], sems.at[k, i - 1]
            )
            copy.start()
            copies.append(copy)

        def sweep(i, before):
            above = [
                pltpu.roll(jnp.where(sub == TILE - 1, p, x), 1, 0)
                for p, x in zip(before[max(i - 1, 0)], before[i])
            ]
            below = [
                pltpu.roll(jnp.where(sub == 0, p, x), TILE - 1, 0)
                for p, x in zip(before[min(i + 1, ntile - 1)], before[i])
            ]
            return [
                (q + (x + (a + b))) * w
                for q, x, a, b, w in zip(losses[i], sides(before[i]), above, below, weights[i])
            ]

        def conduct(i, q):
            losses.append(q)
            scale = place.has_up if i == 0 else place.has_down if i == ntile - 1 else None
            w = [
                pl.reciprocal(4.0 + xcoo[i * TILE : (i + 1) * TILE, col], approx=True) * x
                for col, x in zip(cols, place.inside)
            ]
            weights.append(w if scale is None else [x * scale for x in w])
            levels[0].append([a * b for a, b in zip(q, weights[i])])
            if 0 < i < ntile - 1:
                hand_out(0, i, q)
            for k in range(1, 4):
                ready = [i - k] if i < ntile - 1 else range(i - k, ntile)
                for at in ready:
                    if at >= (1 if start else 0):
                        outer = at in (0, ntile - 1)
                        levels[k].append(None if k == 3 and outer else sweep(at, levels[k - 1]))
                        if k == 3 and not outer:
                            hand_out(1, at, levels[3][at])

        zero = jnp.zeros((TILE, LANES), F32)
        groups = (harmonics + TILE - 1) // TILE
        first = top - MARGIN

        def valid(row):
            if row < MARGIN:
                return "up", place.has_up
            if row >= MARGIN + slab:
                return "down", place.has_down
            return None, None

        for group in range(groups):
            folds = [Fold(sub) for _ in range(nt)]

            def add(row, values):
                totals = [fold.add(x) for fold, x in zip(folds, values)]
                i, at = divmod(row + first, TILE)
                if at < TILE - 1:
                    return
                rows = slice(i * TILE, (i + 1) * TILE)
                if group:
                    totals = [qq[rows, col] + x for col, x in zip(cols, totals)]
                if group == groups - 1:
                    conduct(i, totals)
                else:
                    for col, x in zip(cols, totals):
                        qq[rows, col] = x

            if not start:
                for row in range(-first, 2):
                    add(row, [zero] * nt)
            eddy(
                place, table[group * TILE : (group + 1) * TILE, :], harmonics, start, slab + 2 * MARGIN,
                lambda row: spread(xcur, row + first, nt), lambda row: spread(xcon, row + first, nt),
                valid, rr, rb, hb, add,
            )
            for row in range(slab + 2 * MARGIN - 2, ext - first):
                add(row, [zero] * nt)

        for copy in copies:
            copy.wait()

    @pl.when(lax.axis_index("mesh") == 0)
    def _():
        run(MARGIN)

    @pl.when(lax.axis_index("mesh") > 0)
    def _():
        run(0)


def on_device(current_pattern, conductivity, cooling, harm_order, harm_amp, block_counts):
    slab, total = current_pattern.shape
    harm, mesh = lax.axis_size("harm"), lax.axis_size("mesh")
    width = total // harm
    wide = width + LANES
    chips = harm // 2
    held = -(-harm // TILE) * TILE
    any_space = pl.BlockSpec(memory_space=pl.ANY)
    vmem = pl.BlockSpec(memory_space=pltpu.VMEM)
    smem = pl.BlockSpec(memory_space=pltpu.SMEM)
    shape = lambda *s: jax.ShapeDtypeStruct(s, F32)
    fields = (current_pattern, conductivity, cooling)

    small = pltpu.CompilerParams(vmem_limit_bytes=4 * 2**20)
    in_hbm = lambda x: pltpu.with_memory_space_constraint(x, pltpu.HBM)
    held_vmem = lambda *s: pltpu.VMEM(s, F32)
    params = pl.pallas_call(
        params_kernel,
        out_shape=held_vmem(held, LANES),
        in_specs=[smem] * 3,
        out_specs=vmem,
        compiler_params=small,
        name="params",
    )(harm_order, harm_amp, block_counts)
    edges = pl.pallas_call(
        functools.partial(pack_kernel, width=width),
        out_shape=held_vmem(4 * TILE, wide),
        in_specs=[any_space] * 4,
        out_specs=vmem,
        scratch_shapes=[
            pltpu.VMEM((3, TILE, min(2 * width + 2 * LANES, total)), F32),
            pltpu.SemaphoreType.DMA((3,)),
        ],
        compiler_params=small,
        name="pack",
    )(params, *map(in_hbm, fields))
    axes = ("mesh", "harm")

    def permute(value, target):
        pairs = []
        for m in range(mesh):
            for z in range(chips):
                for c in range(2):
                    tm, tz, tc = target(m, z, c)
                    pairs.append(
                        (m * harm + z * 2 + c, (tm % mesh) * harm + (tz % chips) * 2 + tc)
                    )
        return lax.ppermute(value, axes, pairs)

    def swap(value):
        return permute(value, lambda m, z, c: (m, z, 1 - c))

    def beside(m, z, c):
        if m == (0 if c else mesh - 1):
            return m, z, 1 - c
        return m + (1 - 2 * c), z, c

    known = jnp.maximum(params, swap(params))
    edges, before = lax.optimization_barrier((edges, known))
    got = permute(edges, beside)
    power = chips & (chips - 1) == 0
    steps = [1 << i for i in range(chips.bit_length() - 1)] if power else range(1, chips)
    last = table = before
    for i, step in enumerate(steps):
        before = jnp.maximum(before, last)
        if power:
            table = before
        sent = jnp.tile(table, (1, 2)) if i else table
        hop = lambda m, z, c: (m, z ^ step if power else z + step, c)
        last = permute(sent, hop)[:, :LANES]
    passed = pl.pallas_call(
        pass_kernel,
        out_shape=held_vmem(2 * TILE, wide),
        in_specs=[any_space, vmem],
        out_specs=vmem,
        compiler_params=small,
        name="pass_on",
    )(before, got)
    far = swap(passed)

    tile_cur, tile_con, tile_coo = pl.pallas_call(
        functools.partial(arrange_kernel, width=width),
        out_shape=(held_vmem(slab, wide),) * 3,
        in_specs=[any_space] * 4,
        out_specs=(vmem,) * 3,
        scratch_shapes=[
            pltpu.VMEM((3, slab, min(width + 2 * LANES, total)), F32),
            pltpu.SemaphoreType.DMA((3,)),
        ],
        compiler_params=small,
        name="arrange",
    )(passed, *fields)

    ext = slab + 2 * TILE
    flat = pltpu.VMEM((ext, wide), F32)
    deep = pltpu.VMEM((slab + 2 * MARGIN, TILE, wide), F32)
    before, tile_cur = lax.optimization_barrier((before, tile_cur))
    known = jnp.maximum(before, last)
    return pl.pallas_call(
        functools.partial(loss_kernel, width=width, harmonics=harm),
        out_shape=(shape(slab, width),) * 2,
        in_specs=[vmem] * 6,
        out_specs=(any_space,) * 2,
        scratch_shapes=[flat] * 3
        + [deep] * 3
        + [flat, pltpu.VMEM((2, slab, width), F32), pltpu.SemaphoreType.DMA((2, slab // TILE))],
        compiler_params=pltpu.CompilerParams(vmem_limit_bytes=12 * 2**20),
        name="losses",
    )(known, tile_cur, tile_con, tile_coo, got, far)


def solution(mesh):
    return jax.shard_map(
        on_device,
        mesh=mesh,
        in_specs=(P("mesh", None),) * 3 + (P("harm"),) * 3,
        out_specs=(P("mesh", "harm"), P("mesh", "harm")),
        check_vma=False,
    )
```

```python
import functools

import jax
import jax.numpy as jnp
from jax import lax
from jax.experimental import pallas as pl
from jax.experimental.pallas import tpu as pltpu
from jax.sharding import PartitionSpec as P

LANES = 128
HALF = 64
TILE = 8
BASE_FREQ = 0.1
MARGIN = 5
F32 = jnp.float32


def lane_iota(rows=TILE):
    return lax.broadcasted_iota(jnp.int32, (rows, LANES), 1)


def sublane_iota():
    return lax.broadcasted_iota(jnp.int32, (TILE, LANES), 0)


def side_tile(buf, rows, left, right):
    lanes = lane_iota(rows.size if hasattr(rows, "size") else rows.stop - rows.start)
    after = buf[rows, pl.ds(pl.multiple_of(right, LANES), LANES)]
    before = buf[rows, pl.ds(pl.multiple_of(left, LANES), LANES)]
    return jnp.where(lanes < HALF, after, before)


def lane_gather(x, index):
    return jnp.take_along_axis(x, index, axis=1)


class Columns:
    def __init__(self, n):
        self.n, lanes = n, lane_iota()
        self.columns = [n * lanes + p for p in range(n)]
        if n % 2:
            inverse = pow(n, -1, LANES)
            self.index = [lax.rem(c, LANES) for c in self.columns]
            self.back = [lax.rem(inverse * (lanes - p + LANES), LANES) for p in range(n)]
            phase = lax.rem(lanes, n)
            self.phase = [phase == k for k in range(n)]
        else:
            self.index = [lax.rem(c, LANES) for c in self.columns]
            self.back = [(t * LANES + lanes) // n for t in range(n)]

    def interleave(self, tiles):
        n, out = self.n, []
        for p in range(n):
            if n % 2:
                mixed = tiles[0]
                for t in range(1, n):
                    mixed = jnp.where(self.phase[(p - t * LANES) % n], tiles[t], mixed)
                out.append(lane_gather(mixed, self.index[p]))
            else:
                mixed = lane_gather(tiles[0], self.index[p])
                for t in range(1, n):
                    mixed = jnp.where(
                        self.columns[p] // LANES == t,
                        lane_gather(tiles[t], self.index[p]),
                        mixed,
                    )
                out.append(mixed)
        return out

    def natural(self, tiles, count):
        n, out = self.n, []
        if n % 2:
            tiles = [lane_gather(x, self.back[p]) for p, x in enumerate(tiles)]
        for t in range(count):
            if n % 2:
                mixed = tiles[0]
                for p in range(1, n):
                    mixed = jnp.where(self.phase[(p - t * LANES) % n], tiles[p], mixed)
            else:
                lanes = lane_iota()
                mixed = lane_gather(tiles[0], self.back[t])
                for p in range(1, n):
                    mixed = jnp.where(
                        lax.rem(lanes, n) == p, lane_gather(tiles[p], self.back[t]), mixed
                    )
            out.append(mixed)
        return out


def window(start, size, total):
    begin = jnp.clip(start - LANES, 0, total - size)
    return pl.multiple_of(begin, LANES)


def table_rows(harmonics):
    return 1 if 3 * harmonics <= LANES else 3


def table_place(k, harmonics):
    return (0, k * harmonics) if table_rows(harmonics) == 1 else (k, 0)


def params_kernel(order, amp, count, params, *, harmonics):
    h = lax.axis_index("harm")
    rows = lax.broadcasted_iota(jnp.int32, params.shape, 0)
    lanes = lax.broadcasted_iota(jnp.int32, params.shape, 1)
    value = jnp.zeros(params.shape, jnp.int32)
    for k, ref in enumerate((order, amp, count)):
        row, lane = table_place(k, harmonics)
        value = jnp.where((rows == row) & (lanes == lane + h), ref[0], value)
    params[...] = value.astype(F32)


def pack_kernel(after, cur, con, coo, out, buf, sems, *, width):
    slab, total = cur.shape
    h = lax.axis_index("harm")
    core = lax.rem(h, 2)
    size = buf.shape[2]
    first = (h - core) * width
    begin = window(first, size, total)
    row = pl.multiple_of(jnp.where(core == 0, slab - TILE, 0), TILE)
    copies = [
        pltpu.make_async_copy(
            ref.at[pl.ds(row, TILE), pl.ds(begin, size)], buf.at[i], sems.at[i]
        )
        for i, ref in enumerate((cur, con, coo))
    ]
    for copy in copies:
        copy.start()
    columns = Columns(width // LANES + 1)
    sub = sublane_iota()
    goes_up = core == 0
    shift = jnp.where(goes_up, 3, 5)
    take_cur = jnp.where(goes_up, sub - 3, 4 - sub) >= 0
    for copy in copies:
        copy.wait()
    for part, target in enumerate((core, 1 - core)):
        offset = first + target * width - begin
        left = jnp.maximum(offset - LANES, 0)
        right = jnp.minimum(offset + width, size - LANES)
        fields = []
        for i in range(3):
            tiles = [
                buf[i, :, pl.ds(pl.multiple_of(offset + j * LANES, LANES), LANES)]
                for j in range(width // LANES)
            ]
            tiles.append(side_tile(buf.at[i], slice(0, TILE), left, right))
            fields.append(tiles)
        joined = [
            jnp.where(take_cur, a, pltpu.roll(c, shift, 0))
            for a, c in zip(fields[0], fields[2])
        ]
        for i, tiles in enumerate((joined, fields[1])):
            rows = slice((2 * part + i) * TILE, (2 * part + i + 1) * TILE)
            for j, tile in enumerate(columns.interleave(tiles)):
                out[rows, j * LANES : (j + 1) * LANES] = tile


def arrange_kernel(after, cur, con, coo, cur_out, con_out, coo_out, held, sems, *, width):
    slab, total = cur.shape
    h = lax.axis_index("harm")
    size = held.shape[2]
    begin = window(h * width, size, total)
    copies = [
        pltpu.make_async_copy(ref.at[:, pl.ds(begin, size)], held.at[i], sems.at[i])
        for i, ref in enumerate((cur, con, coo))
    ]
    for copy in copies:
        copy.start()
    offset = h * width - begin
    left = jnp.maximum(offset - LANES, 0)
    right = jnp.minimum(offset + width, size - LANES)
    columns = Columns(width // LANES + 1)
    for i, tile in enumerate((cur_out, con_out, coo_out)):
        copies[i].wait()
        for r in range(0, slab, TILE):
            rows = slice(r, r + TILE)
            pieces = [
                held[i, rows, pl.ds(pl.multiple_of(offset + j * LANES, LANES), LANES)]
                for j in range(width // LANES)
            ]
            pieces.append(side_tile(held.at[i], rows, left, right))
            for j, piece in enumerate(columns.interleave(pieces)):
                tile[rows, j * LANES : (j + 1) * LANES] = piece


def pass_kernel(after, got, passed):
    passed[...] = got[2 * TILE :, :]


def sides(tiles):
    line = [pltpu.roll(tiles[-1], 1, 1), *tiles, pltpu.roll(tiles[0], LANES - 1, 1)]
    return [a + b for a, b in zip(line[:-2], line[2:])]


class Fold:
    def __init__(self, sub):
        self.low = [(sub & shift) == 0 for shift in (1, 2, 4)]
        self.held = [None] * 3

    def add(self, value):
        for level in range(3):
            first, self.held[level] = self.held[level], None
            if first is None:
                self.held[level] = value
                return None
            low = self.low[level]
            value = jnp.where(low, first, value) + pltpu.roll(
                jnp.where(low, value, first), 1 << level, 0
            )
        return value


def load(ref, row, nt):
    return [ref[row, :, j * LANES : (j + 1) * LANES] for j in range(nt)]


def store(ref, row, tiles):
    for j, tile in enumerate(tiles):
        ref[row, :, j * LANES : (j + 1) * LANES] = tile


def spread(ref, row, nt):
    return [
        jnp.broadcast_to(ref[row : row + 1, j * LANES : (j + 1) * LANES], (TILE, LANES))
        for j in range(nt)
    ]


def pair(here, below):
    below = [*below[1:], pltpu.roll(below[0], LANES - 1, 1)]
    return [a + b for a, b in zip(here, below)]


def neighbours(above, here):
    here = [pltpu.roll(here[-1], 1, 1), *here[:-1]]
    return [a + b for a, b in zip(above, here)]


class Place:
    def __init__(self, width):
        self.width, self.nt = width, width // LANES + 1
        self.h, m = lax.axis_index("harm"), lax.axis_index("mesh")
        self.has_up = (m > 0).astype(F32)
        self.has_down = (m < lax.axis_size("mesh") - 1).astype(F32)
        has_left = (self.h > 0).astype(F32)
        has_right = (self.h < lax.axis_size("harm") - 1).astype(F32)
        self.order_of = Columns(self.nt)
        self.inside = [
            jnp.where(c < width, 1.0, jnp.where(c < width + HALF, has_right, has_left))
            for c in self.order_of.columns
        ]

    def first_block(self, j):
        c = self.order_of.columns[j]
        block = jnp.where(c < self.width + HALF, c // LANES, -1)
        return (block + self.h * (self.width // LANES)).astype(F32)

    def edges(self, near, far, put):
        core = lax.rem(self.h, 2)

        @pl.when(core == 0)
        def _():
            put(near, far)

        @pl.when(core == 1)
        def _():
            put(far, near)


def eddy(place, par, harmonics, start, count_rows, source, conductivity, valid, rr, rb, hb, loss_out):
    nt = place.nt
    table, group = par
    order, amp, count = [
        lane_gather(
            jnp.broadcast_to(table[row : row + 1, :], (TILE, LANES)),
            lane + group * TILE + sublane_iota(),
        )
        for row, lane in (table_place(k, harmonics) for k in range(3))
    ]
    omega = BASE_FREQ * order
    quarter = 0.25 * omega
    scale_of_loss = (0.5 / harmonics) * quarter * omega * amp * amp
    masks = [
        jnp.where(count > place.first_block(j), 0.25 * place.inside[j], 0.0)
        for j in range(nt)
    ]
    scaled = {None: masks}

    old = old_pairs = None
    if start:
        zeros = [jnp.zeros((TILE, LANES), F32)] * nt
        store(rb, start - 1, zeros)
        store(hb, start - 1, zeros)
        old = zeros, zeros
    for row in range(start, count_rows):
        name, factor = valid(row)
        if name not in scaled:
            scaled[name] = [k * factor for k in masks]
        src = source(row)
        g = [quarter * x for x in conductivity(row)]
        r = [
            pl.reciprocal(1.0 + x * x, approx=True) * k for x, k in zip(g, scaled[name])
        ]
        re = [a * b for a, b in zip(src, r)]
        him = [a * b for a, b in zip(g, re)]
        if 2 <= row < count_rows - 2:
            store(rr, row, r)
        if old is not None:
            pairs = pair(old[0], re), pair(old[1], him)
            if old_pairs is not None:
                nr = neighbours(old_pairs[0], pairs[0])
                nh = neighbours(old_pairs[1], pairs[1])
                x = [a + b for a, b in zip(old[4], nr)]
                store(rb, row - 1, [k * (a - b * c) for k, a, b, c in zip(old[2], x, old[3], nh)])
                store(hb, row - 1, [k * (b * a + c) for k, a, b, c in zip(old[2], x, old[3], nh)])
            old_pairs = pairs
        old = re, him, r, g, src

    begin = max(start - 1, 1)
    old, old_pairs = (load(rb, begin, nt), load(hb, begin, nt)), None
    for row in range(begin, count_rows - 2):
        new = load(rb, row + 1, nt), load(hb, row + 1, nt)
        pairs = pair(old[0], new[0]), pair(old[1], new[1])
        old = new
        if old_pairs is not None:
            nr = neighbours(old_pairs[0], pairs[0])
            nh = neighbours(old_pairs[1], pairs[1])
            src, con, r = source(row), conductivity(row), load(rr, row, nt)
            losses = []
            for j in range(nt):
                x = src[j] + nr[j]
                losses.append(
                    (scale_of_loss * con[j] * r[j]) * (x * x + nh[j] * nh[j])
                )
            loss_out(row, losses)
        old_pairs = pairs


def loss_kernel(
    table, cur, con, coo, near, far, diss, heat,
    xcur, xcon, xcoo, rr, rb, hb, qq, results, sems, *, width, harmonics,
):
    slab = coo.shape[0]
    top, bottom = TILE, TILE + slab
    ext = slab + 2 * TILE
    place, nt, sub = Place(width), width // LANES + 1, sublane_iota()
    cols = [slice(j * LANES, (j + 1) * LANES) for j in range(nt)]
    xcur[top:bottom, :] = cur[...]
    xcon[top:bottom, :] = con[...]
    xcoo[top:bottom, :] = coo[...]

    def put(up, down):
        xcur[0:TILE, :] = up[:TILE, :]
        xcon[0:TILE, :] = up[TILE : 2 * TILE, :]
        xcoo[0:TILE, :] = jnp.maximum(pltpu.roll(up[:TILE, :], TILE - 3, 0), 0.0)
        xcur[bottom:ext, :] = down[:TILE, :]
        xcon[bottom:ext, :] = down[TILE : 2 * TILE, :]
        xcoo[bottom:ext, :] = jnp.maximum(pltpu.roll(down[:TILE, :], TILE - 5, 0), 0.0)

    place.edges(near, far, put)

    def run(start):
        ntile = ext // TILE
        losses, weights, levels, copies = [], [], [[], [], [], []], []
        if start:
            nothing = [jnp.zeros((TILE, LANES), F32)] * nt
            losses.append(nothing)
            weights.append(nothing)
            for level in levels:
                level.append(nothing)

        def hand_out(k, i, tiles):
            rows = slice((i - 1) * TILE, i * TILE)
            for col, tile in zip(cols, place.order_of.natural(tiles, nt - 1)):
                results[k, rows, col] = tile
            copy = pltpu.make_async_copy(
                results.at[k, rows, :], (diss, heat)[k].at[rows, :], sems.at[k, i - 1]
            )
            copy.start()
            copies.append(copy)

        def sweep(i, before):
            above = [
                pltpu.roll(jnp.where(sub == TILE - 1, p, x), 1, 0)
                for p, x in zip(before[max(i - 1, 0)], before[i])
            ]
            below = [
                pltpu.roll(jnp.where(sub == 0, p, x), TILE - 1, 0)
                for p, x in zip(before[min(i + 1, ntile - 1)], before[i])
            ]
            return [
                (q + (x + (a + b))) * w
                for q, x, a, b, w in zip(losses[i], sides(before[i]), above, below, weights[i])
            ]

        def conduct(i, q):
            losses.append(q)
            scale = place.has_up if i == 0 else place.has_down if i == ntile - 1 else None
            w = [
                pl.reciprocal(4.0 + xcoo[i * TILE : (i + 1) * TILE, col], approx=True) * x
                for col, x in zip(cols, place.inside)
            ]
            weights.append(w if scale is None else [x * scale for x in w])
            levels[0].append([a * b for a, b in zip(q, weights[i])])
            if 0 < i < ntile - 1:
                hand_out(0, i, q)
            for k in range(1, 4):
                ready = [i - k] if i < ntile - 1 else range(i - k, ntile)
                for at in ready:
                    if at >= (1 if start else 0):
                        outer = at in (0, ntile - 1)
                        levels[k].append(None if k == 3 and outer else sweep(at, levels[k - 1]))
                        if k == 3 and not outer:
                            hand_out(1, at, levels[3][at])

        zero = jnp.zeros((TILE, LANES), F32)
        groups = (harmonics + TILE - 1) // TILE
        first = top - MARGIN

        def valid(row):
            if row < MARGIN:
                return "up", place.has_up
            if row >= MARGIN + slab:
                return "down", place.has_down
            return None, None

        for group in range(groups):
            folds = [Fold(sub) for _ in range(nt)]

            def add(row, values):
                totals = [fold.add(x) for fold, x in zip(folds, values)]
                i, at = divmod(row + first, TILE)
                if at < TILE - 1:
                    return
                rows = slice(i * TILE, (i + 1) * TILE)
                if group:
                    totals = [qq[rows, col] + x for col, x in zip(cols, totals)]
                if group == groups - 1:
                    conduct(i, totals)
                else:
                    for col, x in zip(cols, totals):
                        qq[rows, col] = x

            if not start:
                for row in range(-first, 2):
                    add(row, [zero] * nt)
            eddy(
                place, (table, group), harmonics, start, slab + 2 * MARGIN,
                lambda row: spread(xcur, row + first, nt), lambda row: spread(xcon, row + first, nt),
                valid, rr, rb, hb, add,
            )
            for row in range(slab + 2 * MARGIN - 2, ext - first):
                add(row, [zero] * nt)

        for copy in copies:
            copy.wait()

    @pl.when(lax.axis_index("mesh") == 0)
    def _():
        run(MARGIN)

    @pl.when(lax.axis_index("mesh") > 0)
    def _():
        run(0)


def on_device(current_pattern, conductivity, cooling, harm_order, harm_amp, block_counts):
    slab, total = current_pattern.shape
    harm, mesh = lax.axis_size("harm"), lax.axis_size("mesh")
    width = total // harm
    wide = width + LANES
    chips = harm // 2
    any_space = pl.BlockSpec(memory_space=pl.ANY)
    vmem = pl.BlockSpec(memory_space=pltpu.VMEM)
    smem = pl.BlockSpec(memory_space=pltpu.SMEM)
    shape = lambda *s: jax.ShapeDtypeStruct(s, F32)
    fields = (current_pattern, conductivity, cooling)

    small = pltpu.CompilerParams(vmem_limit_bytes=4 * 2**20)
    in_hbm = lambda x: pltpu.with_memory_space_constraint(x, pltpu.HBM)
    held_vmem = lambda *s: pltpu.VMEM(s, F32)
    params = pl.pallas_call(
        functools.partial(params_kernel, harmonics=harm),
        out_shape=held_vmem(table_rows(harm), LANES),
        in_specs=[smem] * 3,
        out_specs=vmem,
        compiler_params=small,
        name="params",
    )(harm_order, harm_amp, block_counts)
    edges = pl.pallas_call(
        functools.partial(pack_kernel, width=width),
        out_shape=held_vmem(4 * TILE, wide),
        in_specs=[any_space] * 4,
        out_specs=vmem,
        scratch_shapes=[
            pltpu.VMEM((3, TILE, min(2 * width + 2 * LANES, total)), F32),
            pltpu.SemaphoreType.DMA((3,)),
        ],
        compiler_params=small,
        name="pack",
    )(params, *map(in_hbm, fields))
    axes = ("mesh", "harm")

    def permute(value, target):
        pairs = []
        for m in range(mesh):
            for z in range(chips):
                for c in range(2):
                    tm, tz, tc = target(m, z, c)
                    pairs.append(
                        (m * harm + z * 2 + c, (tm % mesh) * harm + (tz % chips) * 2 + tc)
                    )
        return lax.ppermute(value, axes, pairs)

    def swap(value):
        return permute(value, lambda m, z, c: (m, z, 1 - c))

    def beside(m, z, c):
        if m == (0 if c else mesh - 1):
            return m, z, 1 - c
        return m + (1 - 2 * c), z, c

    known = jnp.maximum(params, swap(params))
    edges, before = lax.optimization_barrier((edges, known))
    got = permute(edges, beside)
    power = chips & (chips - 1) == 0
    steps = [1 << i for i in range(chips.bit_length() - 1)] if power else range(1, chips)
    last = table = before
    for i, step in enumerate(steps):
        before = jnp.maximum(before, last)
        if power:
            table = before
        sent = jnp.tile(table, (1, 12)) if i else table
        hop = lambda m, z, c: (m, z ^ step if power else z + step, c)
        last = permute(sent, hop)[:, :LANES]
    passed = pl.pallas_call(
        pass_kernel,
        out_shape=held_vmem(2 * TILE, wide),
        in_specs=[any_space, vmem],
        out_specs=vmem,
        compiler_params=small,
        name="pass_on",
    )(before, got)
    far = swap(passed)

    tile_cur, tile_con, tile_coo = pl.pallas_call(
        functools.partial(arrange_kernel, width=width),
        out_shape=(held_vmem(slab, wide),) * 3,
        in_specs=[any_space] * 4,
        out_specs=(vmem,) * 3,
        scratch_shapes=[
            pltpu.VMEM((3, slab, min(width + 2 * LANES, total)), F32),
            pltpu.SemaphoreType.DMA((3,)),
        ],
        compiler_params=small,
        name="arrange",
    )(passed, *fields)

    ext = slab + 2 * TILE
    flat = pltpu.VMEM((ext, wide), F32)
    deep = pltpu.VMEM((slab + 2 * MARGIN, TILE, wide), F32)
    before, tile_cur = lax.optimization_barrier((before, tile_cur))
    known = jnp.maximum(before, last)
    return pl.pallas_call(
        functools.partial(loss_kernel, width=width, harmonics=harm),
        out_shape=(shape(slab, width),) * 2,
        in_specs=[vmem] * 6,
        out_specs=(any_space,) * 2,
        scratch_shapes=[flat] * 3
        + [deep] * 3
        + [flat, pltpu.VMEM((2, slab, width), F32), pltpu.SemaphoreType.DMA((2, slab // TILE))],
        compiler_params=pltpu.CompilerParams(vmem_limit_bytes=12 * 2**20),
        name="losses",
    )(known, tile_cur, tile_con, tile_coo, got, far)


def solution(mesh):
    return jax.shard_map(
        on_device,
        mesh=mesh,
        in_specs=(P("mesh", None),) * 3 + (P("harm"),) * 3,
        out_specs=(P("mesh", "harm"), P("mesh", "harm")),
        check_vma=False,
    )
```

```python
import functools

import jax
import jax.numpy as jnp
from jax import lax
from jax.experimental import pallas as pl
from jax.experimental.pallas import tpu as pltpu
from jax.sharding import PartitionSpec as P

LANES = 128
HALF = 64
TILE = 8
BASE_FREQ = 0.1
MARGIN = 5
F32 = jnp.float32


def lane_iota(rows=TILE):
    return lax.broadcasted_iota(jnp.int32, (rows, LANES), 1)


def sublane_iota():
    return lax.broadcasted_iota(jnp.int32, (TILE, LANES), 0)


def side_tile(buf, rows, left, right):
    lanes = lane_iota(rows.size if hasattr(rows, "size") else rows.stop - rows.start)
    after = buf[rows, pl.ds(pl.multiple_of(right, LANES), LANES)]
    before = buf[rows, pl.ds(pl.multiple_of(left, LANES), LANES)]
    return jnp.where(lanes < HALF, after, before)


def lane_gather(x, index):
    return jnp.take_along_axis(x, index, axis=1)


class Columns:
    def __init__(self, n):
        self.n, lanes = n, lane_iota()
        self.columns = [n * lanes + p for p in range(n)]
        if n % 2:
            inverse = pow(n, -1, LANES)
            self.index = [lax.rem(c, LANES) for c in self.columns]
            self.back = [lax.rem(inverse * (lanes - p + LANES), LANES) for p in range(n)]
            phase = lax.rem(lanes, n)
            self.phase = [phase == k for k in range(n)]
        else:
            self.index = [lax.rem(c, LANES) for c in self.columns]
            self.back = [(t * LANES + lanes) // n for t in range(n)]

    def interleave(self, tiles):
        n, out = self.n, []
        for p in range(n):
            if n % 2:
                mixed = tiles[0]
                for t in range(1, n):
                    mixed = jnp.where(self.phase[(p - t * LANES) % n], tiles[t], mixed)
                out.append(lane_gather(mixed, self.index[p]))
            else:
                mixed = lane_gather(tiles[0], self.index[p])
                for t in range(1, n):
                    mixed = jnp.where(
                        self.columns[p] // LANES == t,
                        lane_gather(tiles[t], self.index[p]),
                        mixed,
                    )
                out.append(mixed)
        return out

    def natural(self, tiles, count):
        n, out = self.n, []
        if n % 2:
            tiles = [lane_gather(x, self.back[p]) for p, x in enumerate(tiles)]
        for t in range(count):
            if n % 2:
                mixed = tiles[0]
                for p in range(1, n):
                    mixed = jnp.where(self.phase[(p - t * LANES) % n], tiles[p], mixed)
            else:
                lanes = lane_iota()
                mixed = lane_gather(tiles[0], self.back[t])
                for p in range(1, n):
                    mixed = jnp.where(
                        lax.rem(lanes, n) == p, lane_gather(tiles[p], self.back[t]), mixed
                    )
            out.append(mixed)
        return out


def window(start, size, total):
    begin = jnp.clip(start - LANES, 0, total - size)
    return pl.multiple_of(begin, LANES)


def table_rows(harmonics):
    return 1 if 3 * harmonics <= LANES else 3


def table_place(k, harmonics):
    return (0, k * harmonics) if table_rows(harmonics) == 1 else (k, 0)


def params_kernel(order, amp, count, params, *, harmonics):
    h = lax.axis_index("harm")
    rows = lax.broadcasted_iota(jnp.int32, params.shape, 0)
    lanes = lax.broadcasted_iota(jnp.int32, params.shape, 1)
    value = jnp.zeros(params.shape, jnp.int32)
    for k, ref in enumerate((order, amp, count)):
        row, lane = table_place(k, harmonics)
        value = jnp.where((rows == row) & (lanes == lane + h), ref[0], value)
    params[...] = value.astype(F32)


def pack_kernel(after, cur, con, coo, out, buf, sems, *, width):
    slab, total = cur.shape
    h = lax.axis_index("harm")
    core = lax.rem(h, 2)
    size = buf.shape[2]
    first = (h - core) * width
    begin = window(first, size, total)
    row = pl.multiple_of(jnp.where(core == 0, slab - TILE, 0), TILE)
    copies = [
        pltpu.make_async_copy(
            ref.at[pl.ds(row, TILE), pl.ds(begin, size)], buf.at[i], sems.at[i]
        )
        for i, ref in enumerate((cur, con, coo))
    ]
    for copy in copies:
        copy.start()
    columns = Columns(width // LANES + 1)
    sub = sublane_iota()
    goes_up = core == 0
    shift = jnp.where(goes_up, 3, 5)
    take_cur = jnp.where(goes_up, sub - 3, 4 - sub) >= 0
    for copy in copies:
        copy.wait()
    for part, target in enumerate((core, 1 - core)):
        offset = first + target * width - begin
        left = jnp.maximum(offset - LANES, 0)
        right = jnp.minimum(offset + width, size - LANES)
        fields = []
        for i in range(3):
            tiles = [
                buf[i, :, pl.ds(pl.multiple_of(offset + j * LANES, LANES), LANES)]
                for j in range(width // LANES)
            ]
            tiles.append(side_tile(buf.at[i], slice(0, TILE), left, right))
            fields.append(tiles)
        joined = [
            jnp.where(take_cur, a, pltpu.roll(c, shift, 0))
            for a, c in zip(fields[0], fields[2])
        ]
        for i, tiles in enumerate((joined, fields[1])):
            rows = slice((2 * part + i) * TILE, (2 * part + i + 1) * TILE)
            for j, tile in enumerate(columns.interleave(tiles)):
                out[rows, j * LANES : (j + 1) * LANES] = tile


def arrange_kernel(after, cur, con, coo, cur_out, con_out, coo_out, held, sems, *, width):
    slab, total = cur.shape
    h = lax.axis_index("harm")
    size = held.shape[2]
    begin = window(h * width, size, total)
    copies = [
        pltpu.make_async_copy(ref.at[:, pl.ds(begin, size)], held.at[i], sems.at[i])
        for i, ref in enumerate((cur, con, coo))
    ]
    for copy in copies:
        copy.start()
    offset = h * width - begin
    left = jnp.maximum(offset - LANES, 0)
    right = jnp.minimum(offset + width, size - LANES)
    columns = Columns(width // LANES + 1)
    for i, tile in enumerate((cur_out, con_out, coo_out)):
        copies[i].wait()
        for r in range(0, slab, TILE):
            rows = slice(r, r + TILE)
            pieces = [
                held[i, rows, pl.ds(pl.multiple_of(offset + j * LANES, LANES), LANES)]
                for j in range(width // LANES)
            ]
            pieces.append(side_tile(held.at[i], rows, left, right))
            for j, piece in enumerate(columns.interleave(pieces)):
                tile[rows, j * LANES : (j + 1) * LANES] = piece


def pass_kernel(after, got, passed):
    passed[...] = got[2 * TILE :, :]


def sides(tiles):
    line = [pltpu.roll(tiles[-1], 1, 1), *tiles, pltpu.roll(tiles[0], LANES - 1, 1)]
    return [a + b for a, b in zip(line[:-2], line[2:])]


class Fold:
    def __init__(self, sub):
        self.low = [(sub & shift) == 0 for shift in (1, 2, 4)]
        self.held = [None] * 3

    def add(self, value):
        for level in range(3):
            first, self.held[level] = self.held[level], None
            if first is None:
                self.held[level] = value
                return None
            low = self.low[level]
            value = jnp.where(low, first, value) + pltpu.roll(
                jnp.where(low, value, first), 1 << level, 0
            )
        return value


def load(ref, row, nt):
    return [ref[row, :, j * LANES : (j + 1) * LANES] for j in range(nt)]


def store(ref, row, tiles):
    for j, tile in enumerate(tiles):
        ref[row, :, j * LANES : (j + 1) * LANES] = tile


def spread(ref, row, nt):
    return [
        jnp.broadcast_to(ref[row : row + 1, j * LANES : (j + 1) * LANES], (TILE, LANES))
        for j in range(nt)
    ]


def pair(here, below):
    below = [*below[1:], pltpu.roll(below[0], LANES - 1, 1)]
    return [a + b for a, b in zip(here, below)]


def neighbours(above, here):
    here = [pltpu.roll(here[-1], 1, 1), *here[:-1]]
    return [a + b for a, b in zip(above, here)]


class Place:
    def __init__(self, width):
        self.width, self.nt = width, width // LANES + 1
        self.h, m = lax.axis_index("harm"), lax.axis_index("mesh")
        self.has_up = (m > 0).astype(F32)
        self.has_down = (m < lax.axis_size("mesh") - 1).astype(F32)
        has_left = (self.h > 0).astype(F32)
        has_right = (self.h < lax.axis_size("harm") - 1).astype(F32)
        self.order_of = Columns(self.nt)
        self.inside = [
            jnp.where(c < width, 1.0, jnp.where(c < width + HALF, has_right, has_left))
            for c in self.order_of.columns
        ]

    def first_block(self, j):
        c = self.order_of.columns[j]
        block = jnp.where(c < self.width + HALF, c // LANES, -1)
        return (block + self.h * (self.width // LANES)).astype(F32)

    def edges(self, near, far, put):
        core = lax.rem(self.h, 2)

        @pl.when(core == 0)
        def _():
            put(near, far)

        @pl.when(core == 1)
        def _():
            put(far, near)


def eddy(place, par, harmonics, start, count_rows, source, conductivity, valid, rr, rb, hb, loss_out):
    nt = place.nt
    table, group = par
    order, amp, count = [
        lane_gather(
            jnp.broadcast_to(table[row : row + 1, :], (TILE, LANES)),
            lane + group * TILE + sublane_iota(),
        )
        for row, lane in (table_place(k, harmonics) for k in range(3))
    ]
    omega = BASE_FREQ * order
    quarter = 0.25 * omega
    scale_of_loss = (0.5 / harmonics) * quarter * omega * amp * amp
    masks = [
        jnp.where(count > place.first_block(j), 0.25 * place.inside[j], 0.0)
        for j in range(nt)
    ]
    scaled = {None: masks}

    old = old_pairs = None
    if start:
        zeros = [jnp.zeros((TILE, LANES), F32)] * nt
        store(rb, start - 1, zeros)
        store(hb, start - 1, zeros)
        old = zeros, zeros
    for row in range(start, count_rows):
        name, factor = valid(row)
        if name not in scaled:
            scaled[name] = [k * factor for k in masks]
        src = source(row)
        g = [quarter * x for x in conductivity(row)]
        r = [
            pl.reciprocal(1.0 + x * x, approx=True) * k for x, k in zip(g, scaled[name])
        ]
        re = [a * b for a, b in zip(src, r)]
        him = [a * b for a, b in zip(g, re)]
        if 2 <= row < count_rows - 2:
            store(rr, row, r)
        if old is not None:
            pairs = pair(old[0], re), pair(old[1], him)
            if old_pairs is not None:
                nr = neighbours(old_pairs[0], pairs[0])
                nh = neighbours(old_pairs[1], pairs[1])
                x = [a + b for a, b in zip(old[4], nr)]
                store(rb, row - 1, [k * (a - b * c) for k, a, b, c in zip(old[2], x, old[3], nh)])
                store(hb, row - 1, [k * (b * a + c) for k, a, b, c in zip(old[2], x, old[3], nh)])
            old_pairs = pairs
        old = re, him, r, g, src

    begin = max(start - 1, 1)
    old, old_pairs = (load(rb, begin, nt), load(hb, begin, nt)), None
    for row in range(begin, count_rows - 2):
        new = load(rb, row + 1, nt), load(hb, row + 1, nt)
        pairs = pair(old[0], new[0]), pair(old[1], new[1])
        old = new
        if old_pairs is not None:
            nr = neighbours(old_pairs[0], pairs[0])
            nh = neighbours(old_pairs[1], pairs[1])
            src, con, r = source(row), conductivity(row), load(rr, row, nt)
            losses = []
            for j in range(nt):
                x = src[j] + nr[j]
                losses.append(
                    (scale_of_loss * con[j] * r[j]) * (x * x + nh[j] * nh[j])
                )
            loss_out(row, losses)
        old_pairs = pairs


def loss_kernel(
    table, cur, con, coo, near, far, diss, heat,
    xcur, xcon, xcoo, rr, rb, hb, qq, results, sems, *, width, harmonics,
):
    slab = coo.shape[0]
    top, bottom = TILE, TILE + slab
    ext = slab + 2 * TILE
    place, nt, sub = Place(width), width // LANES + 1, sublane_iota()
    cols = [slice(j * LANES, (j + 1) * LANES) for j in range(nt)]

    def put(up, down):
        for rows, side, shift in (
            (slice(0, TILE), up, TILE - 3),
            (slice(TILE, 2 * TILE), down, TILE - 5),
        ):
            xcur[rows, :] = side[:TILE, :]
            xcon[rows, :] = side[TILE : 2 * TILE, :]
            xcoo[rows, :] = jnp.maximum(pltpu.roll(side[:TILE, :], shift, 0), 0.0)

    def of_row(own, margins, row):
        if top <= row < bottom:
            return own, row - top
        return margins, row if row < top else row - slab

    place.edges(near, far, put)

    def run(start):
        ntile = ext // TILE
        losses, weights, levels, copies = [], [], [[], [], [], []], []
        if start:
            nothing = [jnp.zeros((TILE, LANES), F32)] * nt
            losses.append(nothing)
            weights.append(nothing)
            for level in levels:
                level.append(nothing)

        def hand_out(k, i, tiles):
            rows = slice((i - 1) * TILE, i * TILE)
            for col, tile in zip(cols, place.order_of.natural(tiles, nt - 1)):
                results[k, rows, col] = tile
            copy = pltpu.make_async_copy(
                results.at[k, rows, :], (diss, heat)[k].at[rows, :], sems.at[k, i - 1]
            )
            copy.start()
            copies.append(copy)

        def sweep(i, before):
            above = [
                pltpu.roll(jnp.where(sub == TILE - 1, p, x), 1, 0)
                for p, x in zip(before[max(i - 1, 0)], before[i])
            ]
            below = [
                pltpu.roll(jnp.where(sub == 0, p, x), TILE - 1, 0)
                for p, x in zip(before[min(i + 1, ntile - 1)], before[i])
            ]
            return [
                (q + (x + (a + b))) * w
                for q, x, a, b, w in zip(losses[i], sides(before[i]), above, below, weights[i])
            ]

        def conduct(i, q):
            losses.append(q)
            scale = place.has_up if i == 0 else place.has_down if i == ntile - 1 else None
            ref, at = of_row(coo, xcoo, i * TILE)
            w = [
                pl.reciprocal(4.0 + ref[at : at + TILE, col], approx=True) * x
                for col, x in zip(cols, place.inside)
            ]
            weights.append(w if scale is None else [x * scale for x in w])
            levels[0].append([a * b for a, b in zip(q, weights[i])])
            if 0 < i < ntile - 1:
                hand_out(0, i, q)
            for k in range(1, 4):
                ready = [i - k] if i < ntile - 1 else range(i - k, ntile)
                for at in ready:
                    if at >= (1 if start else 0):
                        outer = at in (0, ntile - 1)
                        levels[k].append(None if k == 3 and outer else sweep(at, levels[k - 1]))
                        if k == 3 and not outer:
                            hand_out(1, at, levels[3][at])

        zero = jnp.zeros((TILE, LANES), F32)
        groups = (harmonics + TILE - 1) // TILE
        first = top - MARGIN

        def valid(row):
            if row < MARGIN:
                return "up", place.has_up
            if row >= MARGIN + slab:
                return "down", place.has_down
            return None, None

        for group in range(groups):
            folds = [Fold(sub) for _ in range(nt)]

            def add(row, values):
                totals = [fold.add(x) for fold, x in zip(folds, values)]
                i, at = divmod(row + first, TILE)
                if at < TILE - 1:
                    return
                rows = slice(i * TILE, (i + 1) * TILE)
                if group:
                    totals = [qq[rows, col] + x for col, x in zip(cols, totals)]
                if group == groups - 1:
                    conduct(i, totals)
                else:
                    for col, x in zip(cols, totals):
                        qq[rows, col] = x

            if not start:
                for row in range(-first, 2):
                    add(row, [zero] * nt)
            eddy(
                place, (table, group), harmonics, start, slab + 2 * MARGIN,
                lambda row: spread(*of_row(cur, xcur, row + first), nt),
                lambda row: spread(*of_row(con, xcon, row + first), nt),
                valid, rr, rb, hb, add,
            )
            for row in range(slab + 2 * MARGIN - 2, ext - first):
                add(row, [zero] * nt)

        for copy in copies:
            copy.wait()

    @pl.when(lax.axis_index("mesh") == 0)
    def _():
        run(MARGIN)

    @pl.when(lax.axis_index("mesh") > 0)
    def _():
        run(0)


def on_device(current_pattern, conductivity, cooling, harm_order, harm_amp, block_counts):
    slab, total = current_pattern.shape
    harm, mesh = lax.axis_size("harm"), lax.axis_size("mesh")
    width = total // harm
    wide = width + LANES
    chips = harm // 2
    any_space = pl.BlockSpec(memory_space=pl.ANY)
    vmem = pl.BlockSpec(memory_space=pltpu.VMEM)
    smem = pl.BlockSpec(memory_space=pltpu.SMEM)
    shape = lambda *s: jax.ShapeDtypeStruct(s, F32)
    fields = (current_pattern, conductivity, cooling)

    small = pltpu.CompilerParams(vmem_limit_bytes=4 * 2**20)
    in_hbm = lambda x: pltpu.with_memory_space_constraint(x, pltpu.HBM)
    held_vmem = lambda *s: pltpu.VMEM(s, F32)
    params = pl.pallas_call(
        functools.partial(params_kernel, harmonics=harm),
        out_shape=held_vmem(table_rows(harm), LANES),
        in_specs=[smem] * 3,
        out_specs=vmem,
        compiler_params=small,
        name="params",
    )(harm_order, harm_amp, block_counts)
    edges = pl.pallas_call(
        functools.partial(pack_kernel, width=width),
        out_shape=held_vmem(4 * TILE, wide),
        in_specs=[any_space] * 4,
        out_specs=vmem,
        scratch_shapes=[
            pltpu.VMEM((3, TILE, min(2 * width + 2 * LANES, total)), F32),
            pltpu.SemaphoreType.DMA((3,)),
        ],
        compiler_params=small,
        name="pack",
    )(params, *map(in_hbm, fields))
    axes = ("mesh", "harm")

    def permute(value, target):
        pairs = []
        for m in range(mesh):
            for z in range(chips):
                for c in range(2):
                    tm, tz, tc = target(m, z, c)
                    pairs.append(
                        (m * harm + z * 2 + c, (tm % mesh) * harm + (tz % chips) * 2 + tc)
                    )
        return lax.ppermute(value, axes, pairs)

    def swap(value):
        return permute(value, lambda m, z, c: (m, z, 1 - c))

    def beside(m, z, c):
        if m == (0 if c else mesh - 1):
            return m, z, 1 - c
        return m + (1 - 2 * c), z, c

    known = jnp.maximum(params, swap(params))
    edges, before = lax.optimization_barrier((edges, known))
    got = permute(edges, beside)
    power = chips & (chips - 1) == 0
    steps = [1 << i for i in range(chips.bit_length() - 1)] if power else range(1, chips)
    last = table = before
    for i, step in enumerate(steps):
        before = jnp.maximum(before, last)
        if power:
            table = before
        sent = jnp.tile(table, (1, 12)) if i else table
        hop = lambda m, z, c: (m, z ^ step if power else z + step, c)
        last = permute(sent, hop)[:, :LANES]
    passed = pl.pallas_call(
        pass_kernel,
        out_shape=held_vmem(2 * TILE, wide),
        in_specs=[any_space, vmem],
        out_specs=vmem,
        compiler_params=small,
        name="pass_on",
    )(before, got)
    far = swap(passed)

    tile_cur, tile_con, tile_coo = pl.pallas_call(
        functools.partial(arrange_kernel, width=width),
        out_shape=(held_vmem(slab, wide),) * 3,
        in_specs=[any_space] * 4,
        out_specs=(vmem,) * 3,
        scratch_shapes=[
            pltpu.VMEM((3, slab, min(width + 2 * LANES, total)), F32),
            pltpu.SemaphoreType.DMA((3,)),
        ],
        compiler_params=small,
        name="arrange",
    )(passed, *fields)

    ext = slab + 2 * TILE
    flat = pltpu.VMEM((ext, wide), F32)
    deep = pltpu.VMEM((slab + 2 * MARGIN, TILE, wide), F32)
    before, tile_cur = lax.optimization_barrier((before, tile_cur))
    known = jnp.maximum(before, last)
    return pl.pallas_call(
        functools.partial(loss_kernel, width=width, harmonics=harm),
        out_shape=(shape(slab, width),) * 2,
        in_specs=[vmem] * 6,
        out_specs=(any_space,) * 2,
        scratch_shapes=[pltpu.VMEM((2 * TILE, wide), F32)] * 3
        + [deep] * 3
        + [flat, pltpu.VMEM((2, slab, width), F32), pltpu.SemaphoreType.DMA((2, slab // TILE))],
        compiler_params=pltpu.CompilerParams(vmem_limit_bytes=12 * 2**20),
        name="losses",
    )(known, tile_cur, tile_con, tile_coo, got, far)


def solution(mesh):
    return jax.shard_map(
        on_device,
        mesh=mesh,
        in_specs=(P("mesh", None),) * 3 + (P("harm"),) * 3,
        out_specs=(P("mesh", "harm"), P("mesh", "harm")),
        check_vma=False,
    )
```
